512 devices in a mesh: patch: 64 (over z_hi, x, y, core), head: 8 (over z_lo).
Axes of the slice: x: 4, y: 4, z: 16 (z_hi: 2, z_lo: 8; z = z_hi * 8 + z_lo), core: 2. Of those that a mesh axis runs over, the one named last changes fastest.
Arguments:
- query: bfloat16 [1536, 5120], P(('patch', 'head')), may hold values from -300 to 300
- delta_key: float32 [1536, 5120], P(('patch', 'head')), may hold values from -4 to 4
- delta_value: float32 [1536, 5120], P(('patch', 'head')), may hold values from -4 to 4
- base_key: bfloat16 [1536, 5120], P(None, 'head'), may hold values from -8 to 8
- base_value: bfloat16 [1536, 5120], P(None, 'head'), may hold values from -6 to 6
Outputs:
- attended: bfloat16 [1536, 5120], P(('patch', 'head'))
The draws below stay inside these ranges and needn't reach their ends.
All inputs are finite; a program needn't handle non-finite values. Where the reference program divides by a largest or mean magnitude, that divisor is 1e-20 or more.
Results may differ from the reference program's by a relative error of at most 0.04.
Values may be sent and summed in bfloat16 or wider, within the bound.
A program may use at most 64 MiB of HBM per device.

```python
import math
import jax
import jax.numpy as jnp
from jax import lax

D = 5120
HEADS = 40
HEAD_DIM = 128
TOKENS = 1536


def shared_keys(key):
    return jax.random.normal(key, (TOKENS, D), jnp.float32)


def draw_base_key(key, part):
    base = shared_keys(key)
    return jnp.clip(base, -8.0, 8.0).astype(jnp.bfloat16)


def draw_query(key, part):
    key = jax.random.fold_in(key, 5)
    noise = jax.random.normal(key, (TOKENS, D), jnp.float32) * 0.5
    return noise.astype(jnp.bfloat16)


def level_of(key, dims, split, low, top_value):
    factor_of = 1.0
    for axis_at, shards_of in split:
        draws = jax.random.uniform(jax.random.fold_in(jax.random.fold_in(key, 6), axis_at), (shards_of,), jnp.float32, low / len(split), top_value / len(split))
        factor_of = factor_of * jnp.repeat(jnp.exp(draws), dims[axis_at] // shards_of).reshape((-1,) + (1,) * (len(dims) - 1 - axis_at))
    return factor_of


def bell_draw(stream_key, shape, deviation, reach, split=(), kind=jnp.bfloat16):
    values = deviation * jax.random.normal(stream_key, shape, jnp.float32)
    if split:
        values = values * level_of(stream_key, shape, split, -0.22, 0.18)
    return jnp.clip(values, -reach, reach).astype(kind)


def setup_inputs(seed: int = 0) -> dict:
    splits = jax.random.split(jax.random.key(seed), 6)
    return {
        "query": draw_query(jax.random.fold_in(splits[5], 71), 0),
        "delta_key": bell_draw(splits[1], (TOKENS, D), 0.5, 4.0, ((0, 512),), jnp.float32),
        "delta_value": bell_draw(splits[2], (TOKENS, D), 0.5, 4.0, ((0, 512),), jnp.float32),
        "base_key": draw_base_key(jax.random.fold_in(splits[5], 71), 0),
        "base_value": bell_draw(splits[4], (TOKENS, D), 1.0, 6.0, ((1, 8),)),
    }


def encode(delta, head_dim):
    rows_count, features = delta.shape
    blocks = delta.astype(jnp.float32).reshape(rows_count, features // head_dim, head_dim)
    scales = (lax.optimization_barrier(jnp.max(jnp.abs(blocks), axis=2)) + 1e-06).astype(jnp.bfloat16)
    levels = jnp.floor(127.0 * blocks / scales.astype(jnp.float32)[:, :, None] + 0.5)
    codes = jnp.clip(levels, -127.0, 127.0).astype(jnp.bfloat16)
    return (codes.reshape(rows_count, features), scales)

def decode(base, codes, scales, head_dim):
    rows_count, features = codes.shape
    head_count = features // head_dim
    rebuilt = base.astype(jnp.float32).reshape(rows_count, head_count, head_dim)
    steps_size = scales.astype(jnp.float32)[:, :, None] / 127.0
    rebuilt = rebuilt + codes.astype(jnp.float32).reshape(rows_count, head_count, head_dim) * steps_size
    return rebuilt.astype(jnp.bfloat16)

def reference(query, delta_key, delta_value, base_key, base_value):
    code_k, scale_k = encode(delta_key, HEAD_DIM)
    code_v, scale_v = encode(delta_value, HEAD_DIM)
    keys = decode(base_key, code_k, scale_k, HEAD_DIM)
    values = decode(base_value, code_v, scale_v, HEAD_DIM)
    queries = query.reshape(TOKENS, HEADS, HEAD_DIM)
    factor = 1.0 / math.sqrt(HEAD_DIM)

    def one_head(triple):
        q_head, k_head, v_head = triple
        scores = jnp.dot(q_head, k_head.T, preferred_element_type=jnp.float32) * factor
        peak = lax.optimization_barrier(jnp.max(scores, axis=1))
        weights = jnp.exp(scores - peak[:, None])
        row_total = lax.optimization_barrier(jnp.sum(weights, axis=1))
        mixed = jnp.dot(weights.astype(jnp.bfloat16), v_head, preferred_element_type=jnp.float32)
        return mixed / row_total[:, None]
    stacked = (queries.transpose(1, 0, 2), keys.transpose(1, 0, 2), values.transpose(1, 0, 2))
    result = lax.map(one_head, stacked)
    return result.transpose(1, 0, 2).reshape(TOKENS, D).astype(jnp.bfloat16)
```

```python
import math

import jax
import jax.numpy as jnp
from jax import lax
from jax.experimental import pallas as pl
from jax.experimental.pallas import tpu as pltpu
from jax.sharding import PartitionSpec as P

MESH = pl.DeviceIdType.MESH
F32 = jnp.float32
BF16 = jnp.bfloat16

HD = 128
NX, NY, NC = 4, 4, 2
NL = 8
NZ = 2 * NL
TOK = 3
ZT = TOK * NZ
HT = TOK * NL
YC = NY * NC
PLANE = NX * YC
MSG = 32
KEYS = NX * ZT
SLOTS = 128
OROWS = HD + 16
SCALE2 = math.log2(math.e) / math.sqrt(HD)

NT = (((1,), (1,)), ((), ()))


def kernel(
    q_ref, dk_ref, dv_ref, bk_ref, bv_ref, out_ref,
    stage, sbuf, rbuf, pmat, p2mat, bwin, bf32,
    kall, vall, qall, vt, obuf, orecv, fbuf, frecv, fstage, fout,
    bsem, zs, zr, ks, kr, vs, vr, qs, qr, osm, orm, fs, fr,
):
    p = lax.axis_index("patch")
    h = lax.axis_index("head")
    zh = lax.div(p, PLANE)
    xyc = lax.rem(p, PLANE)
    x = lax.div(xyc, YC)
    yc = lax.rem(xyc, YC)
    y = lax.div(yc, NC)
    core = lax.rem(yc, NC)
    z = zh * NL + h

    def zdev(z2):
        return (lax.div(z2, NL) * PLANE + xyc, lax.rem(z2, NL))

    def xdev(x2):
        return (zh * PLANE + x2 * YC + yc, h)

    def ydev(yc2):
        return (zh * PLANE + x * YC + yc2, h)

    barrier = pltpu.get_barrier_semaphore()

    @pl.loop(1, NZ)
    def _(k):
        pl.semaphore_signal(barrier, inc=1, device_id=zdev(lax.rem(z + k, NZ)), device_id_type=MESH)

    @pl.loop(1, NX)
    def _(k):
        pl.semaphore_signal(barrier, inc=1, device_id=xdev(lax.rem(x + k, NX)), device_id_type=MESH)

    @pl.loop(1, YC)
    def _(k):
        pl.semaphore_signal(barrier, inc=1, device_id=ydev(lax.rem(yc + k, YC)), device_id_type=MESH)

    base_copies = []
    for a, ref in enumerate((bk_ref, bv_ref)):
        for half in range(2):
            row0 = pl.multiple_of(lax.div(HT * (xyc + half * PLANE), 16) * 16, 16)
            rows = pl.ds(row0, 32)
            ab = pl.ds(pl.multiple_of(zh * (3 * HD), HD), 2 * HD)
            n = 2 * (2 * a + half)
            base_copies.append(pltpu.make_async_copy(
                ref.at[rows, ab], bwin.at[a, half, :, pl.ds(0, 2 * HD)], bsem.at[n]))
            base_copies.append(pltpu.make_async_copy(
                ref.at[rows, pl.ds(2 * HD, HD)], bwin.at[a, half, :, pl.ds(2 * HD, HD)], bsem.at[n + 1]))
    for copy in base_copies:
        copy.start()

    lane = lax.broadcasted_iota(jnp.int32, (TOK, HD), 1)
    stage[:, 30:32, :] = jnp.zeros((NZ, 2, HD), F32)

    def encode(ref, g):
        block = ref[:, g * HD:(g + 1) * HD]
        scale = (jnp.max(jnp.abs(block), axis=1, keepdims=True) + 1e-06).astype(BF16).astype(F32)
        levels = jnp.floor(127.0 * block / scale + 0.5)
        return jnp.clip(levels, -127.0, 127.0), scale

    for hd in range(NL):
        scales = [jnp.zeros((TOK, HD), F32), jnp.zeros((TOK, HD), F32)]
        for j in range(5):
            g = 5 * hd + j
            code_k, scale_k = encode(dk_ref, g)
            code_v, scale_v = encode(dv_ref, g)
            query = q_ref[:, g * HD:(g + 1) * HD].astype(F32)
            targets = ((0, j),) if j < 2 else (((0, 2), (1, 2)) if j == 2 else ((1, j - 3),))
            for zz, slot in targets:
                dst = zz * NL + hd
                for n, piece in ((slot, code_k), (3 + slot, code_v), (6 + slot, query)):
                    stage[dst, 3 * n:3 * n + 3, :] = piece
                scales[zz] = jnp.where(lane == slot, scale_k, scales[zz])
                scales[zz] = jnp.where(lane == 3 + slot, scale_v, scales[zz])
        for zz in range(2):
            dst = zz * NL + hd
            stage[dst, 27:30, :] = scales[zz]
            sbuf[dst] = stage[dst].astype(BF16)

    pl.semaphore_wait(barrier, (NZ - 1) + (NX - 1) + (YC - 1))

    def zcopy(z2, mine, theirs):
        return pltpu.make_async_remote_copy(
            src_ref=sbuf.at[z2], dst_ref=rbuf.at[mine], send_sem=zs.at[z2], recv_sem=zr.at[theirs],
            device_id=zdev(z2), device_id_type=MESH)

    @pl.loop(1, NZ)
    def _(k):
        zcopy(lax.rem(z + k, NZ), z, z).start()

    rbuf[z] = sbuf[z]

    col = lax.broadcasted_iota(jnp.int32, (1, NZ * MSG), 1)
    row_in = jnp.bitwise_and(col, MSG - 1)
    piece_of = jnp.right_shift(row_in * 43, 7)
    token_of = 3 * jnp.right_shift(col, 5) + row_in - 3 * piece_of
    key = token_of + ZT * piece_of
    for n in range(10):
        r = lax.broadcasted_iota(jnp.int32, (ZT, NZ * MSG), 0) + n * ZT
        pmat[n * ZT:(n + 1) * ZT, :] = jnp.where(r == key, 1.0, 0.0).astype(BF16)
    r = lax.broadcasted_iota(jnp.int32, (32, NZ * MSG), 0) + (8 * ZT + HT * zh)
    pmat[10 * ZT:10 * ZT + 32, :] = jnp.where(r == key, 1.0, 0.0).astype(BF16)

    r2 = lax.broadcasted_iota(jnp.int32, (NZ * 16, SLOTS), 0)
    s2 = lax.broadcasted_iota(jnp.int32, (NZ * 16, SLOTS), 1)
    owner = jnp.right_shift(r2, 4)
    rr = jnp.bitwise_and(r2, 15)
    slot_a = jnp.where(rr < 3, 3 * owner + rr, -1)
    slot_b = jnp.where((rr >= 8) & (rr < 11), ZT + 3 * owner + rr - 8, -1)
    near = (rr >= 4) & (rr < 7) & (jnp.right_shift(owner, 3) == zh)
    slot_c = jnp.where(near, 2 * ZT + 3 * jnp.bitwise_and(owner, 7) + rr - 4, -1)
    p2mat[...] = jnp.where((s2 == slot_a) | (s2 == slot_b) | (s2 == slot_c), 1.0, 0.0).astype(BF16)

    for copy in base_copies:
        copy.wait()
    bf32[...] = bwin[...].astype(F32)

    @pl.loop(1, NZ)
    def _(k):
        z2 = lax.rem(z + k, NZ)
        zcopy(z2, z, z2).wait_recv()

    arrived = rbuf[...].reshape(NZ * MSG, HD)

    def pick(first, rows):
        return jnp.dot(pmat[first:first + rows, :], arrived, preferred_element_type=F32)

    steps = pick(9 * ZT, ZT) / 127.0
    shift = pl.ds(pl.multiple_of(8 * lax.rem(xyc, 2), 8), HT)

    def decode(a, dest):
        for slot in range(3):
            codes = pick((3 * a + slot) * ZT, ZT)
            step = steps[:, 3 * a + slot:3 * a + slot + 1]
            base = jnp.concatenate(
                [bf32[a, half, shift, slot * HD:(slot + 1) * HD] for half in range(2)], axis=0)
            dest[slot, x] = (base + codes * step).astype(BF16)

    def xcopy(buf, x2, mine, theirs, ssem, rsem):
        return pltpu.make_async_remote_copy(
            src_ref=buf.at[:, mine], dst_ref=buf.at[:, mine], send_sem=ssem.at[x2], recv_sem=rsem.at[theirs],
            device_id=xdev(x2), device_id_type=MESH)

    def ycopy(src, dst, yc2, theirs, ssem, rsem):
        return pltpu.make_async_remote_copy(
            src_ref=src, dst_ref=dst, send_sem=ssem.at[yc2], recv_sem=rsem.at[theirs],
            device_id=ydev(yc2), device_id_type=MESH)

    decode(0, kall)

    @pl.loop(1, NX)
    def _(k):
        xcopy(kall, lax.rem(x + k, NX), x, x, ks, kr).start()

    qall[yc] = jnp.concatenate([pick(6 * ZT, 2 * ZT), pick(10 * ZT, 32)], axis=0).astype(BF16)

    @pl.loop(1, YC)
    def _(k):
        yc2 = lax.rem(yc + k, YC)
        ycopy(qall.at[yc], qall.at[yc], yc2, yc, qs, qr).start()

    decode(1, vall)

    @pl.loop(1, NX)
    def _(k):
        xcopy(vall, lax.rem(x + k, NX), x, x, vs, vr).start()

    @pl.loop(1, NX)
    def _(k):
        x2 = lax.rem(x + k, NX)
        xcopy(kall, x2, x2, x2, ks, kr).wait_recv()

    @pl.loop(1, NX)
    def _(k):
        x2 = lax.rem(x + k, NX)
        xcopy(vall, x2, x2, x2, vs, vr).wait_recv()

    eye = jnp.where(
        lax.broadcasted_iota(jnp.int32, (HD, HD), 0) == lax.broadcasted_iota(jnp.int32, (HD, HD), 1),
        1.0, 0.0).astype(BF16)
    for slot in range(3):
        values = vall[slot].reshape(KEYS, HD)
        vt[slot * HD:(slot + 1) * HD, :] = lax.dot_general(
            eye, values, NT, preferred_element_type=F32).astype(BF16)

    slot_lane = jnp.bitwise_and(lax.broadcasted_iota(jnp.int32, (1, NC * SLOTS), 1), SLOTS - 1)
    in_a, in_b = slot_lane < ZT, slot_lane < 2 * ZT
    stat_row = lax.broadcasted_iota(jnp.int32, (16, NC * SLOTS), 0)

    def choose(stacked, rows):
        return jnp.where(
            in_a, stacked[0:rows], jnp.where(in_b, stacked[rows:2 * rows], stacked[2 * rows:3 * rows]))

    def attend(y2):
        first = y2 * NC
        queries = qall[pl.ds(first, NC)].reshape(NC * SLOTS, HD)
        keys = kall[...].reshape(3 * KEYS, HD)
        scores = lax.dot_general(keys, queries, NT, preferred_element_type=F32)
        scores = choose(scores, KEYS) * SCALE2
        peak = jnp.max(scores, axis=0, keepdims=True)
        peak_hi = peak.astype(BF16).astype(F32)
        peak_lo = (peak - peak_hi).astype(BF16).astype(F32)
        weights = jnp.exp2(scores - (peak_hi + peak_lo))
        total = jnp.sum(weights, axis=0, keepdims=True)
        total_hi = total.astype(BF16).astype(F32)
        total_lo = total - total_hi
        mixed = jnp.dot(vt[...], weights.astype(BF16), preferred_element_type=F32)
        mixed = choose(mixed, HD).astype(BF16)
        stats = jnp.where(stat_row == 0, peak_hi, jnp.where(
            stat_row == 1, peak_lo, jnp.where(
                stat_row == 2, total_hi, jnp.where(stat_row == 3, total_lo, 0.0)))).astype(BF16)
        for c in range(NC):
            obuf[first + c, 0:HD, :] = mixed[:, c * SLOTS:(c + 1) * SLOTS]
            obuf[first + c, HD:OROWS, :] = stats[:, c * SLOTS:(c + 1) * SLOTS]

    def send_out(yc2):
        ycopy(obuf.at[yc2], orecv.at[yc], yc2, yc, osm, orm).start()

    def wait_queries(yc2):
        ycopy(qall.at[yc2], qall.at[yc2], yc2, yc2, qs, qr).wait_recv()

    wait_queries(y * NC + 1 - core)
    attend(y)
    send_out(y * NC + 1 - core)
    orecv[yc] = obuf[yc]

    @pl.loop(1, NY)
    def _(k):
        y2 = lax.rem(y + k, NY)
        for c in range(NC):
            wait_queries(y2 * NC + c)
        attend(y2)
        for c in range(NC):
            send_out(y2 * NC + c)

    @pl.loop(1, YC)
    def _(k):
        yc2 = lax.rem(yc + k, YC)
        ycopy(obuf.at[yc2], orecv.at[yc2], yc2, yc2, osm, orm).wait_recv()

    stats = [orecv[n, HD:OROWS, :].astype(F32) for n in range(YC)]
    peaks = [s[0:1] + s[1:2] for s in stats]
    top = peaks[0]
    for n in range(1, YC):
        top = jnp.maximum(top, peaks[n])
    parts = [jnp.exp2(peaks[n] - top) for n in range(YC)]
    total = jnp.zeros((1, SLOTS), F32)
    for n in range(YC):
        total = total + parts[n] * (stats[n][2:3] + stats[n][3:4])
    joined = jnp.zeros((HD, SLOTS), F32)
    for n in range(YC):
        joined = joined + orecv[n, 0:HD, :].astype(F32) * parts[n]
    joined = (joined / total).astype(BF16)
    owned = lax.dot_general(p2mat[...], joined, NT, preferred_element_type=F32)
    fbuf[...] = owned.astype(BF16).reshape(NZ, 16, HD)

    def fcopy(z2, mine, theirs):
        return pltpu.make_async_remote_copy(
            src_ref=fbuf.at[z2], dst_ref=frecv.at[mine], send_sem=fs.at[z2], recv_sem=fr.at[theirs],
            device_id=zdev(z2), device_id_type=MESH)

    @pl.loop(1, NZ)
    def _(k):
        fcopy(lax.rem(z + k, NZ), z, z).start()

    frecv[z] = fbuf[z]

    @pl.loop(1, NZ)
    def _(k):
        z2 = lax.rem(z + k, NZ)
        zcopy(z2, z, z2).wait_send()

    @pl.loop(1, NX)
    def _(k):
        x2 = lax.rem(x + k, NX)
        xcopy(kall, x2, x, x2, ks, kr).wait_send()
        xcopy(vall, x2, x, x2, vs, vr).wait_send()

    @pl.loop(1, YC)
    def _(k):
        yc2 = lax.rem(yc + k, YC)
        ycopy(qall.at[yc], qall.at[yc], yc2, yc2, qs, qr).wait_send()
        ycopy(obuf.at[yc2], orecv.at[yc], yc2, yc2, osm, orm).wait_send()

    @pl.loop(1, NZ)
    def _(k):
        z2 = lax.rem(z + k, NZ)
        fcopy(z2, z2, z2).wait_recv()

    fstage[...] = frecv[...].astype(F32)
    for n in range(NZ):
        g = 5 * (n % NL) + 3 * (n // NL)
        fout[:, g * HD:(g + 1) * HD] = fstage[n, 0:3, :]
        fout[:, (g + 1) * HD:(g + 2) * HD] = fstage[n, 8:11, :]
    for hd in range(NL):
        g = 5 * hd + 2
        fout[:, g * HD:(g + 1) * HD] = fstage[zh * NL + hd, 4:7, :]
    out_ref[...] = fout[...].astype(BF16)

    @pl.loop(1, NZ)
    def _(k):
        z2 = lax.rem(z + k, NZ)
        fcopy(z2, z, z2).wait_send()


def on_device(query, delta_key, delta_value, base_key, base_value):
    vmem = pl.BlockSpec(memory_space=pltpu.VMEM)
    hbm = pl.BlockSpec(memory_space=pl.ANY)
    dma = pltpu.SemaphoreType.DMA
    return pl.pallas_call(
        kernel,
        out_shape=jax.ShapeDtypeStruct(query.shape, BF16),
        in_specs=[vmem, vmem, vmem, hbm, hbm],
        out_specs=vmem,
        scratch_shapes=[
            pltpu.VMEM((NZ, MSG, HD), F32),
            pltpu.VMEM((NZ, MSG, HD), BF16),
            pltpu.VMEM((NZ, MSG, HD), BF16),
            pltpu.VMEM((10 * ZT + 32, NZ * MSG), BF16),
            pltpu.VMEM((NZ * 16, SLOTS), BF16),
            pltpu.VMEM((2, 2, 32, 3 * HD), BF16),
            pltpu.VMEM((2, 2, 32, 3 * HD), F32),
            pltpu.VMEM((3, NX, ZT, HD), BF16),
            pltpu.VMEM((3, NX, ZT, HD), BF16),
            pltpu.VMEM((YC, SLOTS, HD), BF16),
            pltpu.VMEM((3 * HD, KEYS), BF16),
            pltpu.VMEM((YC, OROWS, SLOTS), BF16),
            pltpu.VMEM((YC, OROWS, SLOTS), BF16),
            pltpu.VMEM((NZ, 16, HD), BF16),
            pltpu.VMEM((NZ, 16, HD), BF16),
            pltpu.VMEM((NZ, 16, HD), F32),
            pltpu.VMEM(query.shape, F32),
            dma((8,)), dma((NZ,)), dma((NZ,)), dma((NX,)), dma((NX,)), dma((NX,)), dma((NX,)),
            dma((YC,)), dma((YC,)), dma((YC,)), dma((YC,)), dma((NZ,)), dma((NZ,)),
        ],
        compiler_params=pltpu.CompilerParams(
            collective_id=0, has_side_effects=True, vmem_limit_bytes=60 * 1024 * 1024),
    )(query, delta_key, delta_value, base_key, base_value)


def solution(mesh):
    rows = P(("patch", "head"), None)
    cols = P(None, "head")
    return jax.shard_map(
        on_device, mesh=mesh, in_specs=(rows, rows, rows, cols, cols), out_specs=rows, check_vma=False)
```

```python
import math

import jax
import jax.numpy as jnp
from jax import lax
from jax.experimental import pallas as pl
from jax.experimental.pallas import tpu as pltpu
from jax.sharding import PartitionSpec as P

MESH = pl.DeviceIdType.MESH
F32 = jnp.float32
BF16 = jnp.bfloat16

HD = 128
NX, NY, NC = 4, 4, 2
NL = 8
NZ = 2 * NL
GH = 5
GW = GH * HD
TOK = 3
ZT = TOK * NZ
HT = TOK * NL
NXY = NX * NY
PLANE = NXY * NC
KEYS = NC * ZT
SLOTS = 128
OROWS = HD + 16
REACH = (4, -3, 3, -2, 2, -1, 1)
SCALE2 = math.log2(math.e) / math.sqrt(HD)

NT = (((1,), (1,)), ((), ()))


def iota(shape, dim):
    return lax.broadcasted_iota(jnp.int32, shape, dim)


def one_hot(cond):
    return jnp.where(cond, 1.0, 0.0).astype(BF16)


def third(n):
    return jnp.right_shift(n * 43, 7)


def slot_of(r):
    rr = jnp.bitwise_and(r, 15)
    j = third(rr)
    slot = HT * j + TOK * jnp.right_shift(r, 4) + rr - 3 * j
    return jnp.where(rr < 15, slot, -1)


def kernel(
    q_ref, dk_ref, dv_ref, bk_ref, bv_ref, out_ref,
    stage, qstage, sbuf, qsend, rbuf, qrecv, pmat, bwin, bf32,
    kall, vall, qall, vt, obuf, orecv, fbuf, frecv, fstage, fout,
    bsem, zs, zr, ws, wr, cs, cr, qs, qr, osm, orm, fs, fr,
):
    p = lax.axis_index("patch")
    h = lax.axis_index("head")
    zh = lax.div(p, PLANE)
    xyc = lax.rem(p, PLANE)
    xy = lax.div(xyc, NC)
    core = lax.rem(xyc, NC)
    z = zh * NL + h

    def zdev(z2):
        return (lax.div(z2, NL) * PLANE + xyc, lax.rem(z2, NL))

    def pdev(xy2):
        return (zh * PLANE + xy2 * NC + core, h)

    def zfar(k):
        half = lax.div(k + 1, 2)
        return lax.rem(z + NL + (2 * lax.rem(k, 2) - 1) * half + NZ, NZ)

    def near(d):
        return lax.rem(z + d + NZ, NZ)

    def cdev():
        return (zh * PLANE + xy * NC + 1 - core, h)

    barrier = pltpu.get_barrier_semaphore()

    @pl.loop(0, NZ - 1)
    def _(k):
        pl.semaphore_signal(barrier, inc=1, device_id=zdev(zfar(k)), device_id_type=MESH)

    @pl.loop(1, NXY)
    def _(k):
        pl.semaphore_signal(barrier, inc=1, device_id=pdev(lax.rem(xy + k, NXY)), device_id_type=MESH)

    pl.semaphore_signal(barrier, inc=1, device_id=cdev(), device_id_type=MESH)

    base_copies = []
    for a, ref in enumerate((bk_ref, bv_ref)):
        for half in range(2):
            row0 = pl.multiple_of(lax.div(HT * (xyc + half * PLANE), 16) * 16, 16)
            base_copies.append(pltpu.make_async_copy(
                ref.at[pl.ds(row0, 32)], bwin.at[a, half], bsem.at[2 * a + half]))
    for copy in base_copies:
        copy.start()

    lane = iota((TOK, HD), 1)
    sub = iota((TOK, HD), 0)
    qstage[:, 15:16, :] = jnp.zeros((NL, 1, HD), F32)

    def encode(ref, g):
        block = ref[:, g * HD:(g + 1) * HD]
        scale = (jnp.max(jnp.abs(block), axis=1, keepdims=True) + 1e-06).astype(BF16).astype(F32)
        levels = jnp.floor(127.0 * block / scale + 0.5)
        return jnp.clip(levels, -127.0, 127.0), scale

    for hd in range(NL):
        for a, ref in enumerate((dk_ref, dv_ref)):
            scales = jnp.zeros((TOK, HD), F32)
            for j in range(GH):
                code, scale = encode(ref, GH * hd + j)
                stage[hd, 16 * a + 3 * j:16 * a + 3 * j + 3, :] = code
                scales = jnp.where(lane == 3 * j + sub, scale, scales)
            stage[hd, 16 * a + 15:16 * a + 16, :] = jnp.sum(scales, axis=0, keepdims=True)
        sbuf[hd] = stage[hd].astype(BF16)

    for hd in range(NL):
        for j in range(GH):
            g = GH * hd + j
            qstage[hd, 3 * j:3 * j + 3, :] = q_ref[:, g * HD:(g + 1) * HD].astype(F32)
    qsend[...] = qstage[...].astype(BF16)

    pl.semaphore_wait(barrier, (NZ - 1) + (NXY - 1) + 1)

    def zcopy(z2, mine, theirs):
        return pltpu.make_async_remote_copy(
            src_ref=sbuf.at[lax.rem(z2, NL)], dst_ref=rbuf.at[mine], send_sem=zs.at[z2], recv_sem=zr.at[theirs],
            device_id=zdev(z2), device_id_type=MESH)

    def wcopy(d):
        i, z2 = d + 3, near(-d)
        return pltpu.make_async_remote_copy(
            src_ref=qsend.at[lax.rem(z2, NL)], dst_ref=qrecv.at[i], send_sem=ws.at[i], recv_sem=wr.at[i],
            device_id=zdev(z2), device_id_type=MESH)

    @pl.loop(0, NZ - 1)
    def _(k):
        zcopy(zfar(k), z, z).start()

    for d in REACH:
        wcopy(d).start()

    rbuf[z] = sbuf[h]
    qrecv[3] = qsend[h]

    col = iota((1, NZ * 32), 1)
    src = jnp.right_shift(col, 5)
    row32 = jnp.bitwise_and(col, 31)
    row16 = jnp.bitwise_and(col, 15)
    kind = jnp.right_shift(row32, 4)
    j_of = third(row16)
    key = kind * (GH * ZT) + ZT * j_of + TOK * src + row16 - 3 * j_of
    key = jnp.where(row16 < 15, key, -1)
    for n in range(2 * GH):
        pmat[n * ZT:(n + 1) * ZT, :] = one_hot(iota((ZT, NZ * 32), 0) + n * ZT == key)
    token = iota((ZT, NZ * 32), 0) - TOK * src
    mine = (token >= 0) & (token < TOK)
    for a in range(2):
        pmat[(2 * GH + a) * ZT:(2 * GH + a + 1) * ZT, :] = one_hot(mine & (row32 == 16 * a + 15))
    to_slots = one_hot(iota((SLOTS, NL * 16), 0) == slot_of(iota((SLOTS, NL * 16), 1)))
    to_owners = one_hot(slot_of(iota((NL * 16, SLOTS), 0)) == iota((NL * 16, SLOTS), 1))

    for d in REACH:
        wcopy(d).wait_recv()
    qall[xy] = jnp.dot(
        to_slots, qrecv[...].reshape(NL * 16, HD), preferred_element_type=F32).astype(BF16)

    def pcopy(src, dst, xy2, theirs, ssem, rsem):
        return pltpu.make_async_remote_copy(
            src_ref=src, dst_ref=dst, send_sem=ssem.at[xy2], recv_sem=rsem.at[theirs],
            device_id=pdev(xy2), device_id_type=MESH)

    @pl.loop(1, NXY)
    def _(k):
        xy2 = lax.rem(xy + k, NXY)
        pcopy(qall.at[xy], qall.at[xy], xy2, xy, qs, qr).start()

    for copy in base_copies:
        copy.wait()
    bf32[...] = bwin[...].astype(F32)

    @pl.loop(0, NZ - 1)
    def _(k):
        z2 = zfar(NZ - 2 - k)
        zcopy(z2, z, z2).wait_recv()

    arrived = rbuf[...].reshape(NZ * 32, HD)
    scales = jnp.dot(pmat[2 * GH * ZT:, :], arrived, preferred_element_type=F32)
    token_in = iota((ZT, HD), 0)
    lane_of = iota((ZT, HD), 1) - (token_in - 3 * third(token_in))
    picked = [
        jnp.where(lane_of == 3 * j, scales[a * ZT:(a + 1) * ZT], 0.0).astype(BF16)
        for a in range(2) for j in range(GH)]
    steps = jnp.dot(
        jnp.concatenate(picked, axis=0), jnp.ones((HD, HD), BF16), preferred_element_type=F32) / 127.0
    shift = pl.ds(pl.multiple_of(8 * lax.rem(xyc, 2), 8), HT)

    def decode(a, j, codes):
        n = a * GH + j
        base = jnp.concatenate(
            [bf32[a, half, shift, j * HD:(j + 1) * HD] for half in range(2)], axis=0)
        return (base + codes[j * ZT:(j + 1) * ZT] * steps[n * ZT:(n + 1) * ZT]).astype(BF16)

    def ccopy(a, mine, theirs):
        buf = (kall, vall)[a]
        return pltpu.make_async_remote_copy(
            src_ref=buf.at[:, mine], dst_ref=buf.at[:, mine], send_sem=cs.at[a], recv_sem=cr.at[a],
            device_id=cdev(), device_id_type=MESH)

    for a, buf in enumerate((kall, vall)):
        codes = jnp.dot(pmat[a * GH * ZT:(a + 1) * GH * ZT, :], arrived, preferred_element_type=F32)
        for j in range(GH):
            buf[j, core] = decode(a, j, codes)
        ccopy(a, core, core).start()
    for a in range(2):
        ccopy(a, core, core).wait_recv()

    eye = one_hot(iota((HD, HD), 0) == iota((HD, HD), 1))
    vt[...] = lax.dot_general(
        eye, vall[...].reshape(GH * KEYS, HD), NT, preferred_element_type=F32).astype(BF16)

    slot_lane = jnp.bitwise_and(iota((1, 2 * SLOTS), 1), SLOTS - 1)
    stat_row = iota((16, 2 * SLOTS), 0)

    def attend(m):
        queries = qall[pl.ds(2 * m, 2)].reshape(2 * SLOTS, HD)
        stacked = lax.dot_general(
            kall[...].reshape(GH * KEYS, HD), queries, NT, preferred_element_type=F32)
        scores = stacked[(GH - 1) * KEYS:]
        for j in range(GH - 2, -1, -1):
            scores = jnp.where(slot_lane < HT * (j + 1), stacked[j * KEYS:(j + 1) * KEYS], scores)
        scores = scores * SCALE2
        peak = jnp.max(scores, axis=0, keepdims=True)
        peak_hi = peak.astype(BF16).astype(F32)
        peak_lo = (peak - peak_hi).astype(BF16).astype(F32)
        weights = jnp.exp2(scores - (peak_hi + peak_lo))
        total = jnp.sum(weights, axis=0, keepdims=True)
        total_hi = total.astype(BF16).astype(F32)
        total_lo = total - total_hi
        by_head = []
        for j in range(GH):
            in_head = slot_lane >= HT * j
            if j < GH - 1:
                in_head = in_head & (slot_lane < HT * (j + 1))
            by_head.append(jnp.where(in_head, weights, 0.0).astype(BF16))
        mixed = jnp.dot(
            vt[...], jnp.concatenate(by_head, axis=0), preferred_element_type=F32).astype(BF16)
        stats = jnp.where(stat_row == 0, peak_hi, jnp.where(
            stat_row == 1, peak_lo, jnp.where(
                stat_row == 2, total_hi, jnp.where(stat_row == 3, total_lo, 0.0)))).astype(BF16)
        for c in range(2):
            obuf[2 * m + c, 0:HD, :] = mixed[:, c * SLOTS:(c + 1) * SLOTS]
            obuf[2 * m + c, HD:OROWS, :] = stats[:, c * SLOTS:(c + 1) * SLOTS]

    pairs = NXY // 2

    @pl.loop(0, pairs)
    def _(k):
        turn = (2 * lax.rem(k, 2) - 1) * lax.div(k + 1, 2)
        m = lax.rem(lax.div(xy, 2) + pairs // 2 + turn + pairs, pairs)
        for c in range(2):
            tile = 2 * m + c

            @pl.when(tile != xy)
            def _():
                pcopy(qall.at[tile], qall.at[tile], tile, tile, qs, qr).wait_recv()

        attend(m)
        for c in range(2):
            tile = 2 * m + c

            @pl.when(tile != xy)
            def _():
                pcopy(obuf.at[tile], orecv.at[xy], tile, xy, osm, orm).start()

            @pl.when(tile == xy)
            def _():
                orecv[tile] = obuf[tile]

    @pl.loop(1, NXY)
    def _(k):
        xy2 = lax.rem(xy + k, NXY)
        pcopy(obuf.at[xy2], orecv.at[xy2], xy2, xy2, osm, orm).wait_recv()

    stats = [orecv[n, HD:OROWS, :].astype(F32) for n in range(NXY)]
    peaks = [s[0:1] + s[1:2] for s in stats]
    top = peaks[0]
    for n in range(1, NXY):
        top = jnp.maximum(top, peaks[n])
    parts = [jnp.exp2(peaks[n] - top) for n in range(NXY)]
    total = jnp.zeros((1, SLOTS), F32)
    for n in range(NXY):
        total = total + parts[n] * (stats[n][2:3] + stats[n][3:4])
    joined = jnp.zeros((HD, SLOTS), F32)
    for n in range(NXY):
        joined = joined + orecv[n, 0:HD, :].astype(F32) * parts[n]
    joined = (joined / total).astype(BF16)
    owned = lax.dot_general(to_owners, joined, NT, preferred_element_type=F32)
    fbuf[...] = owned.astype(BF16).reshape(NL, 16, HD)

    def fcopy(d, theirs):
        i, z2 = d + 3, near(d)
        return pltpu.make_async_remote_copy(
            src_ref=fbuf.at[i], dst_ref=frecv.at[h], send_sem=fs.at[i], recv_sem=fr.at[theirs],
            device_id=zdev(z2), device_id_type=MESH)

    for d in REACH:
        fcopy(d, h).start()

    frecv[h] = fbuf[3]

    @pl.loop(0, NZ - 1)
    def _(k):
        zcopy(zfar(k), z, z).wait_send()

    for d in REACH:
        wcopy(d).wait_send()

    for a in range(2):
        ccopy(a, core, core).wait_send()

    @pl.loop(1, NXY)
    def _(k):
        xy2 = lax.rem(xy + k, NXY)
        pcopy(qall.at[xy], qall.at[xy], xy2, xy2, qs, qr).wait_send()
        pcopy(obuf.at[xy2], orecv.at[xy], xy2, xy2, osm, orm).wait_send()

    @pl.loop(1, NL)
    def _(k):
        h2 = lax.rem(h + k, NL)
        pltpu.make_async_remote_copy(
            src_ref=fbuf.at[0], dst_ref=frecv.at[h2], send_sem=fs.at[0], recv_sem=fr.at[h2],
            device_id=zdev(near(1)), device_id_type=MESH).wait_recv()

    fstage[...] = frecv[...].astype(F32)
    for hd in range(NL):
        for j in range(GH):
            g = GH * hd + j
            fout[:, g * HD:(g + 1) * HD] = fstage[hd, 3 * j:3 * j + 3, :]
    out_ref[...] = fout[...].astype(BF16)

    for d in REACH:
        fcopy(d, h).wait_send()


def on_device(query, delta_key, delta_value, base_key, base_value):
    vmem = pl.BlockSpec(memory_space=pltpu.VMEM)
    hbm = pl.BlockSpec(memory_space=pl.ANY)
    dma = pltpu.SemaphoreType.DMA
    return pl.pallas_call(
        kernel,
        out_shape=jax.ShapeDtypeStruct(query.shape, BF16),
        in_specs=[vmem, vmem, vmem, hbm, hbm],
        out_specs=vmem,
        scratch_shapes=[
            pltpu.VMEM((NL, 32, HD), F32),
            pltpu.VMEM((NL, 16, HD), F32),
            pltpu.VMEM((NL, 32, HD), BF16),
            pltpu.VMEM((NL, 16, HD), BF16),
            pltpu.VMEM((NZ, 32, HD), BF16),
            pltpu.VMEM((NL, 16, HD), BF16),
            pltpu.VMEM(((2 * GH + 2) * ZT, NZ * 32), BF16),
            pltpu.VMEM((2, 2, 32, GW), BF16),
            pltpu.VMEM((2, 2, 32, GW), F32),
            pltpu.VMEM((GH, NC, ZT, HD), BF16),
            pltpu.VMEM((GH, NC, ZT, HD), BF16),
            pltpu.VMEM((NXY, SLOTS, HD), BF16),
            pltpu.VMEM((HD, GH * KEYS), BF16),
            pltpu.VMEM((NXY, OROWS, SLOTS), BF16),
            pltpu.VMEM((NXY, OROWS, SLOTS), BF16),
            pltpu.VMEM((NL, 16, HD), BF16),
            pltpu.VMEM((NL, 16, HD), BF16),
            pltpu.VMEM((NL, 16, HD), F32),
            pltpu.VMEM(query.shape, F32),
            dma((4,)), dma((NZ,)), dma((NZ,)), dma((NL,)), dma((NL,)), dma((2,)), dma((2,)),
            dma((NXY,)), dma((NXY,)), dma((NXY,)), dma((NXY,)), dma((NL,)), dma((NL,)),
        ],
        compiler_params=pltpu.CompilerParams(
            collective_id=0, has_side_effects=True, vmem_limit_bytes=60 * 1024 * 1024),
    )(query, delta_key, delta_value, base_key, base_value)


def solution(mesh):
    rows = P(("patch", "head"), None)
    cols = P(None, "head")
    return jax.shard_map(
        on_device, mesh=mesh, in_specs=(rows, rows, rows, cols, cols), out_specs=rows, check_vma=False)
```

```python
import math

import jax
import jax.numpy as jnp
from jax import lax
from jax.experimental import pallas as pl
from jax.experimental.pallas import tpu as pltpu
from jax.sharding import PartitionSpec as P

MESH = pl.DeviceIdType.MESH
F32 = jnp.float32
BF16 = jnp.bfloat16

HD = 128
NX, NY, NC = 4, 4, 2
NL = 8
NZ = 2 * NL
GH = 5
GW = GH * HD
TOK = 3
ZT = TOK * NZ
HT = TOK * NL
NXY = NX * NY
PLANE = NXY * NC
KEYS = NC * ZT
SLOTS = 128
OROWS = HD + 16
REACH = (4, -3, 3, -2, 2, -1, 1)
SCALE2 = math.log2(math.e) / math.sqrt(HD)

NT = (((1,), (1,)), ((), ()))


def iota(shape, dim):
    return lax.broadcasted_iota(jnp.int32, shape, dim)


def one_hot(cond):
    return jnp.where(cond, 1.0, 0.0).astype(BF16)


def third(n):
    return jnp.right_shift(n * 43, 7)


def slot_of(r):
    rr = jnp.bitwise_and(r, 15)
    j = third(rr)
    slot = HT * j + TOK * jnp.right_shift(r, 4) + rr - 3 * j
    return jnp.where(rr < 15, slot, -1)


def kernel(
    q_ref, dk_ref, dv_ref, bk_ref, bv_ref, out_ref,
    stage, qstage, sbuf, qsend, rbuf, qrecv, pmat, bwin, bf32,
    kall, vall, qall, vt, obuf, orecv, fbuf, frecv, fstage, fout, q_in, dk_in, dv_in,
    isem, bsem, zs, zr, ws, wr, cs, cr, qs, qr, osm, orm, fs, fr,
):
    p = lax.axis_index("patch")
    h = lax.axis_index("head")
    zh = lax.div(p, PLANE)
    xyc = lax.rem(p, PLANE)
    xy = lax.div(xyc, NC)
    core = lax.rem(xyc, NC)
    z = zh * NL + h

    def zdev(z2):
        return (lax.div(z2, NL) * PLANE + xyc, lax.rem(z2, NL))

    def pfar(k):
        turn_x = lax.div(k, NY)
        turn_y = lax.rem(k, NY)
        x2 = lax.rem(lax.div(xy, NY) + NX // 2 + (2 * lax.rem(turn_x, 2) - 1) * lax.div(turn_x + 1, 2) + NX, NX)
        y2 = lax.rem(lax.rem(xy, NY) + NY // 2 + (2 * lax.rem(turn_y, 2) - 1) * lax.div(turn_y + 1, 2) + NY, NY)
        return x2 * NY + y2

    def pdev(xy2):
        return (zh * PLANE + xy2 * NC + core, h)

    def zfar(k):
        half = lax.div(k + 1, 2)
        return lax.rem(z + NL + (2 * lax.rem(k, 2) - 1) * half + NZ, NZ)

    def near(d):
        return lax.rem(z + d + NZ, NZ)

    def cdev():
        return (zh * PLANE + xy * NC + 1 - core, h)

    barrier = pltpu.get_barrier_semaphore()

    @pl.loop(0, NZ - 1)
    def _(k):
        pl.semaphore_signal(barrier, inc=1, device_id=zdev(zfar(k)), device_id_type=MESH)

    @pl.loop(1, NXY)
    def _(k):
        pl.semaphore_signal(barrier, inc=1, device_id=pdev(lax.rem(xy + k, NXY)), device_id_type=MESH)

    pl.semaphore_signal(barrier, inc=1, device_id=cdev(), device_id_type=MESH)

    base_copies = []
    for a, ref in enumerate((bk_ref, bv_ref)):
        for half in range(2):
            row0 = pl.multiple_of(lax.div(HT * (xyc + half * PLANE), 16) * 16, 16)
            base_copies.append(pltpu.make_async_copy(
                ref.at[pl.ds(row0, 32)], bwin.at[a, half], bsem.at[2 * a + half]))
    in_copies = [
        pltpu.make_async_copy(src, dst, isem.at[n])
        for n, (src, dst) in enumerate(((dk_ref, dk_in), (dv_ref, dv_in), (q_ref, q_in)))]
    for copy in in_copies:
        copy.start()
    for copy in base_copies:
        copy.start()

    lane = iota((TOK, HD), 1)
    sub = iota((TOK, HD), 0)
    for copy in in_copies:
        copy.wait()
    qstage[:, 15:16, :] = jnp.zeros((NL, 1, HD), F32)

    def encode(ref, g):
        block = ref[:, g * HD:(g + 1) * HD]
        scale = (jnp.max(jnp.abs(block), axis=1, keepdims=True) + 1e-06).astype(BF16).astype(F32)
        levels = jnp.floor(127.0 * block / scale + 0.5)
        return jnp.clip(levels, -127.0, 127.0), scale

    for hd in range(NL):
        for a, ref in enumerate((dk_in, dv_in)):
            scales = jnp.zeros((TOK, HD), F32)
            for j in range(GH):
                code, scale = encode(ref, GH * hd + j)
                stage[hd, 16 * a + 3 * j:16 * a + 3 * j + 3, :] = code
                scales = jnp.where(lane == 3 * j + sub, scale, scales)
            stage[hd, 16 * a + 15:16 * a + 16, :] = jnp.sum(scales, axis=0, keepdims=True)
        sbuf[hd] = stage[hd].astype(BF16)

    for hd in range(NL):
        for j in range(GH):
            g = GH * hd + j
            qstage[hd, 3 * j:3 * j + 3, :] = q_in[:, g * HD:(g + 1) * HD].astype(F32)
    qsend[...] = qstage[...].astype(BF16)

    pl.semaphore_wait(barrier, (NZ - 1) + (NXY - 1) + 1)

    def zcopy(z2, mine, theirs):
        return pltpu.make_async_remote_copy(
            src_ref=sbuf.at[lax.rem(z2, NL)], dst_ref=rbuf.at[mine], send_sem=zs.at[z2], recv_sem=zr.at[theirs],
            device_id=zdev(z2), device_id_type=MESH)

    def wcopy(d):
        i, z2 = d + 3, near(-d)
        return pltpu.make_async_remote_copy(
            src_ref=qsend.at[lax.rem(z2, NL)], dst_ref=qrecv.at[i], send_sem=ws.at[i], recv_sem=wr.at[i],
            device_id=zdev(z2), device_id_type=MESH)

    for d in REACH:
        wcopy(d).start()

    @pl.loop(0, NZ - 1)
    def _(k):
        zcopy(zfar(k), z, z).start()

    rbuf[z] = sbuf[h]
    qrecv[3] = qsend[h]

    col = iota((1, NZ * 32), 1)
    src = jnp.right_shift(col, 5)
    row32 = jnp.bitwise_and(col, 31)
    row16 = jnp.bitwise_and(col, 15)
    kind = jnp.right_shift(row32, 4)
    j_of = third(row16)
    key = kind * (GH * ZT) + ZT * j_of + TOK * src + row16 - 3 * j_of
    key = jnp.where(row16 < 15, key, -1)
    for n in range(2 * GH):
        pmat[n * ZT:(n + 1) * ZT, :] = one_hot(iota((ZT, NZ * 32), 0) + n * ZT == key)
    token = iota((ZT, NZ * 32), 0) - TOK * src
    mine = (token >= 0) & (token < TOK)
    for a in range(2):
        pmat[(2 * GH + a) * ZT:(2 * GH + a + 1) * ZT, :] = one_hot(mine & (row32 == 16 * a + 15))
    to_slots = one_hot(iota((SLOTS, NL * 16), 0) == slot_of(iota((SLOTS, NL * 16), 1)))
    to_owners = one_hot(slot_of(iota((NL * 16, SLOTS), 0)) == iota((NL * 16, SLOTS), 1))

    for d in REACH:
        wcopy(d).wait_recv()
    qall[xy] = jnp.dot(
        to_slots, qrecv[...].reshape(NL * 16, HD), preferred_element_type=F32).astype(BF16)

    def pcopy(src, dst, xy2, theirs, ssem, rsem):
        return pltpu.make_async_remote_copy(
            src_ref=src, dst_ref=dst, send_sem=ssem.at[xy2], recv_sem=rsem.at[theirs],
            device_id=pdev(xy2), device_id_type=MESH)

    @pl.loop(0, NXY - 1)
    def _(k):
        pcopy(qall.at[xy], qall.at[xy], pfar(k), xy, qs, qr).start()

    for copy in base_copies:
        copy.wait()
    bf32[...] = bwin[...].astype(F32)

    @pl.loop(0, NZ - 1)
    def _(k):
        z2 = zfar(NZ - 2 - k)
        zcopy(z2, z, z2).wait_recv()

    arrived = rbuf[...].reshape(NZ * 32, HD)
    scales = jnp.dot(pmat[2 * GH * ZT:, :], arrived, preferred_element_type=F32)
    token_in = iota((ZT, HD), 0)
    lane_of = iota((ZT, HD), 1) - (token_in - 3 * third(token_in))
    picked = [
        jnp.where(lane_of == 3 * j, scales[a * ZT:(a + 1) * ZT], 0.0).astype(BF16)
        for a in range(2) for j in range(GH)]
    steps = jnp.dot(
        jnp.concatenate(picked, axis=0), jnp.ones((HD, HD), BF16), preferred_element_type=F32) / 127.0
    shift = pl.ds(pl.multiple_of(8 * lax.rem(xyc, 2), 8), HT)

    def decode(a, j, codes):
        n = a * GH + j
        base = jnp.concatenate(
            [bf32[a, half, shift, j * HD:(j + 1) * HD] for half in range(2)], axis=0)
        return (base + codes[j * ZT:(j + 1) * ZT] * steps[n * ZT:(n + 1) * ZT]).astype(BF16)

    def ccopy(a, mine, theirs):
        buf = (kall, vall)[a]
        return pltpu.make_async_remote_copy(
            src_ref=buf.at[:, mine], dst_ref=buf.at[:, mine], send_sem=cs.at[a], recv_sem=cr.at[a],
            device_id=cdev(), device_id_type=MESH)

    for a, buf in enumerate((kall, vall)):
        codes = jnp.dot(pmat[a * GH * ZT:(a + 1) * GH * ZT, :], arrived, preferred_element_type=F32)
        for j in range(GH):
            buf[j, core] = decode(a, j, codes)
        ccopy(a, core, core).start()
    for a in range(2):
        ccopy(a, core, core).wait_recv()

    eye = one_hot(iota((HD, HD), 0) == iota((HD, HD), 1))
    vt[...] = lax.dot_general(
        eye, vall[...].reshape(GH * KEYS, HD), NT, preferred_element_type=F32).astype(BF16)

    slot_lane = jnp.bitwise_and(iota((1, 2 * SLOTS), 1), SLOTS - 1)
    stat_row = iota((16, 2 * SLOTS), 0)

    def attend(m):
        queries = qall[pl.ds(2 * m, 2)].reshape(2 * SLOTS, HD)
        stacked = lax.dot_general(
            kall[...].reshape(GH * KEYS, HD), queries, NT, preferred_element_type=F32)
        scores = stacked[(GH - 1) * KEYS:]
        for j in range(GH - 2, -1, -1):
            scores = jnp.where(slot_lane < HT * (j + 1), stacked[j * KEYS:(j + 1) * KEYS], scores)
        scores = scores * SCALE2
        peak = jnp.max(scores, axis=0, keepdims=True)
        peak_hi = peak.astype(BF16).astype(F32)
        peak_lo = (peak - peak_hi).astype(BF16).astype(F32)
        weights = jnp.exp2(scores - (peak_hi + peak_lo))
        total = jnp.sum(weights, axis=0, keepdims=True)
        total_hi = total.astype(BF16).astype(F32)
        total_lo = total - total_hi
        by_head = []
        for j in range(GH):
            in_head = slot_lane >= HT * j
            if j < GH - 1:
                in_head = in_head & (slot_lane < HT * (j + 1))
            by_head.append(jnp.where(in_head, weights, 0.0).astype(BF16))
        mixed = jnp.dot(
            vt[...], jnp.concatenate(by_head, axis=0), preferred_element_type=F32).astype(BF16)
        stats = jnp.where(stat_row == 0, peak_hi, jnp.where(
            stat_row == 1, peak_lo, jnp.where(
                stat_row == 2, total_hi, jnp.where(stat_row == 3, total_lo, 0.0)))).astype(BF16)
        for c in range(2):
            obuf[2 * m + c, 0:HD, :] = mixed[:, c * SLOTS:(c + 1) * SLOTS]
            obuf[2 * m + c, HD:OROWS, :] = stats[:, c * SLOTS:(c + 1) * SLOTS]

    pairs = NXY // 2

    @pl.loop(0, pairs)
    def _(k):
        turn = (2 * lax.rem(k, 2) - 1) * lax.div(k + 1, 2)
        m = lax.rem(lax.div(xy, 2) + pairs // 2 + turn + pairs, pairs)
        for c in range(2):
            tile = 2 * m + c

            @pl.when(tile != xy)
            def _():
                pcopy(qall.at[tile], qall.at[tile], tile, tile, qs, qr).wait_recv()

        attend(m)
        for c in range(2):
            tile = 2 * m + c

            @pl.when(tile != xy)
            def _():
                pcopy(obuf.at[tile], orecv.at[xy], tile, xy, osm, orm).start()

            @pl.when(tile == xy)
            def _():
                orecv[tile] = obuf[tile]

    @pl.loop(1, NXY)
    def _(k):
        xy2 = lax.rem(xy + k, NXY)
        pcopy(obuf.at[xy2], orecv.at[xy2], xy2, xy2, osm, orm).wait_recv()

    stats = [orecv[n, HD:OROWS, :].astype(F32) for n in range(NXY)]
    peaks = [s[0:1] + s[1:2] for s in stats]
    top = peaks[0]
    for n in range(1, NXY):
        top = jnp.maximum(top, peaks[n])
    parts = [jnp.exp2(peaks[n] - top) for n in range(NXY)]
    total = jnp.zeros((1, SLOTS), F32)
    for n in range(NXY):
        total = total + parts[n] * (stats[n][2:3] + stats[n][3:4])
    joined = jnp.zeros((HD, SLOTS), F32)
    for n in range(NXY):
        joined = joined + orecv[n, 0:HD, :].astype(F32) * parts[n]
    joined = (joined / total).astype(BF16)
    owned = lax.dot_general(to_owners, joined, NT, preferred_element_type=F32)
    fbuf[...] = owned.astype(BF16).reshape(NL, 16, HD)

    def fcopy(d, theirs):
        i, z2 = d + 3, near(d)
        return pltpu.make_async_remote_copy(
            src_ref=fbuf.at[i], dst_ref=frecv.at[h], send_sem=fs.at[i], recv_sem=fr.at[theirs],
            device_id=zdev(z2), device_id_type=MESH)

    for d in REACH:
        fcopy(d, h).start()

    frecv[h] = fbuf[3]

    @pl.loop(0, NZ - 1)
    def _(k):
        zcopy(zfar(k), z, z).wait_send()

    for d in REACH:
        wcopy(d).wait_send()

    for a in range(2):
        ccopy(a, core, core).wait_send()

    @pl.loop(1, NXY)
    def _(k):
        xy2 = lax.rem(xy + k, NXY)
        pcopy(qall.at[xy], qall.at[xy], xy2, xy2, qs, qr).wait_send()
        pcopy(obuf.at[xy2], orecv.at[xy], xy2, xy2, osm, orm).wait_send()

    @pl.loop(1, NL)
    def _(k):
        h2 = lax.rem(h + k, NL)
        pltpu.make_async_remote_copy(
            src_ref=fbuf.at[0], dst_ref=frecv.at[h2], send_sem=fs.at[0], recv_sem=fr.at[h2],
            device_id=zdev(near(1)), device_id_type=MESH).wait_recv()

    fstage[...] = frecv[...].astype(F32)
    for hd in range(NL):
        for j in range(GH):
            g = GH * hd + j
            fout[:, g * HD:(g + 1) * HD] = fstage[hd, 3 * j:3 * j + 3, :]
    out_ref[...] = fout[...].astype(BF16)

    for d in REACH:
        fcopy(d, h).wait_send()


def on_device(query, delta_key, delta_value, base_key, base_value):
    vmem = pl.BlockSpec(memory_space=pltpu.VMEM)
    hbm = pl.BlockSpec(memory_space=pl.ANY)
    dma = pltpu.SemaphoreType.DMA
    return pl.pallas_call(
        kernel,
        out_shape=jax.ShapeDtypeStruct(query.shape, BF16),
        in_specs=[hbm] * 5,
        out_specs=vmem,
        scratch_shapes=[
            pltpu.VMEM((NL, 32, HD), F32),
            pltpu.VMEM((NL, 16, HD), F32),
            pltpu.VMEM((NL, 32, HD), BF16),
            pltpu.VMEM((NL, 16, HD), BF16),
            pltpu.VMEM((NZ, 32, HD), BF16),
            pltpu.VMEM((NL, 16, HD), BF16),
            pltpu.VMEM(((2 * GH + 2) * ZT, NZ * 32), BF16),
            pltpu.VMEM((2, 2, 32, GW), BF16),
            pltpu.VMEM((2, 2, 32, GW), F32),
            pltpu.VMEM((GH, NC, ZT, HD), BF16),
            pltpu.VMEM((GH, NC, ZT, HD), BF16),
            pltpu.VMEM((NXY, SLOTS, HD), BF16),
            pltpu.VMEM((HD, GH * KEYS), BF16),
            pltpu.VMEM((NXY, OROWS, SLOTS), BF16),
            pltpu.VMEM((NXY, OROWS, SLOTS), BF16),
            pltpu.VMEM((NL, 16, HD), BF16),
            pltpu.VMEM((NL, 16, HD), BF16),
            pltpu.VMEM((NL, 16, HD), F32),
            pltpu.VMEM(query.shape, F32),
            pltpu.VMEM(query.shape, BF16),
            pltpu.VMEM(query.shape, F32),
            pltpu.VMEM(query.shape, F32),
            dma((3,)), dma((4,)), dma((NZ,)), dma((NZ,)), dma((NL,)), dma((NL,)), dma((2,)), dma((2,)),
            dma((NXY,)), dma((NXY,)), dma((NXY,)), dma((NXY,)), dma((NL,)), dma((NL,)),
        ],
        compiler_params=pltpu.CompilerParams(
            collective_id=0, has_side_effects=True, vmem_limit_bytes=60 * 1024 * 1024),
    )(query, delta_key, delta_value, base_key, base_value)


def solution(mesh):
    rows = P(("patch", "head"), None)
    cols = P(None, "head")
    return jax.shard_map(
        on_device, mesh=mesh, in_specs=(rows, rows, rows, cols, cols), out_specs=rows, check_vma=False)
```

```python
import math

import jax
import jax.numpy as jnp
from jax import lax
from jax.experimental import pallas as pl
from jax.experimental.pallas import tpu as pltpu
from jax.sharding import PartitionSpec as P

MESH = pl.DeviceIdType.MESH
F32 = jnp.float32
BF16 = jnp.bfloat16

HD = 128
NX, NY, NC = 4, 4, 2
NL = 8
NZ = 2 * NL
GH = 5
GW = GH * HD
TOK = 3
ZT = TOK * NZ
HT = TOK * NL
NXY = NX * NY
PLANE = NXY * NC
KEYS = NC * ZT
NP = NL // 2
SLOTS = 64
QUAD = 4
REACH = (4, -3, 3, -2, 2, -1, 1)
SCALE2 = math.log2(math.e) / math.sqrt(HD)

NT = (((1,), (1,)), ((), ()))


def iota(shape, dim):
    return lax.broadcasted_iota(jnp.int32, shape, dim)


def one_hot(cond):
    return jnp.where(cond, 1.0, 0.0).astype(BF16)


def third(n):
    return jnp.right_shift(n * 43, 7)


def slot_of(r):
    rr = jnp.bitwise_and(r, 15)
    j = third(rr)
    slot = NP * TOK * j + TOK * jnp.right_shift(r, 4) + rr - 3 * j
    return jnp.where(rr < 15, slot, -1)


def place(home, d):
    return lax.rem(d + 3 + jnp.minimum(lax.rem(home + 5, NZ), NL), NL)


def owner_at(home, pos):
    return lax.rem(pos - jnp.minimum(lax.rem(home + 5, NZ), NL) + NL, NL) - 3


def kernel(
    q_ref, dk_ref, dv_ref, bk_ref, bv_ref, out_ref,
    stage, qstage, sbuf, qsend, rbuf, qrecv, pmat, bwin, bf32,
    kall, vall, qall, vt, pbuf, stbuf, obuf, orecv, coef, fbuf, frecv, fstage, fout, q_in, dk_in, dv_in,
    isem, bsem, zs, zr, ws, wr, cs, cr, qs, qr, osm, orm, fs, fr,
):
    p = lax.axis_index("patch")
    h = lax.axis_index("head")
    zh = lax.div(p, PLANE)
    xyc = lax.rem(p, PLANE)
    xy = lax.div(xyc, NC)
    core = lax.rem(xyc, NC)
    z = zh * NL + h

    def zdev(z2):
        return (lax.div(z2, NL) * PLANE + xyc, lax.rem(z2, NL))

    def pfar(k):
        turn_x = lax.div(k, NY)
        turn_y = lax.rem(k, NY)
        x2 = lax.rem(lax.div(xy, NY) + NX // 2 + (2 * lax.rem(turn_x, 2) - 1) * lax.div(turn_x + 1, 2) + NX, NX)
        y2 = lax.rem(lax.rem(xy, NY) + NY // 2 + (2 * lax.rem(turn_y, 2) - 1) * lax.div(turn_y + 1, 2) + NY, NY)
        return x2 * NY + y2

    def pdev(xy2):
        return (zh * PLANE + xy2 * NC + core, h)

    def zfar(k):
        half = lax.div(k + 1, 2)
        return lax.rem(z + NL + (2 * lax.rem(k, 2) - 1) * half + NZ, NZ)

    def near(d):
        return lax.rem(z + d + NZ, NZ)

    def cdev():
        return (zh * PLANE + xy * NC + 1 - core, h)

    barrier = pltpu.get_barrier_semaphore()

    @pl.loop(0, NZ - 1)
    def _(k):
        pl.semaphore_signal(barrier, inc=1, device_id=zdev(zfar(k)), device_id_type=MESH)

    @pl.loop(1, NXY)
    def _(k):
        pl.semaphore_signal(barrier, inc=1, device_id=pdev(lax.rem(xy + k, NXY)), device_id_type=MESH)

    pl.semaphore_signal(barrier, inc=1, device_id=cdev(), device_id_type=MESH)

    base_copies = []
    for a, ref in enumerate((bk_ref, bv_ref)):
        for half in range(2):
            row0 = pl.multiple_of(lax.div(HT * (xyc + half * PLANE), 16) * 16, 16)
            base_copies.append(pltpu.make_async_copy(
                ref.at[pl.ds(row0, 32)], bwin.at[a, half], bsem.at[2 * a + half]))
    in_copies = [
        pltpu.make_async_copy(src, dst, isem.at[n])
        for n, (src, dst) in enumerate(((dk_ref, dk_in), (dv_ref, dv_in), (q_ref, q_in)))]
    for copy in in_copies:
        copy.start()
    for copy in base_copies:
        copy.start()

    lane = iota((TOK, HD), 1)
    sub = iota((TOK, HD), 0)
    for copy in in_copies:
        copy.wait()
    qstage[:, 15:16, :] = jnp.zeros((NL, 1, HD), F32)

    def encode(ref, g):
        block = ref[:, g * HD:(g + 1) * HD]
        scale = (jnp.max(jnp.abs(block), axis=1, keepdims=True) + 1e-06).astype(BF16).astype(F32)
        levels = jnp.floor(127.0 * block / scale + 0.5)
        return jnp.clip(levels, -127.0, 127.0), scale

    for hd in range(NL):
        for a, ref in enumerate((dk_in, dv_in)):
            scales = jnp.zeros((TOK, HD), F32)
            for j in range(GH):
                code, scale = encode(ref, GH * hd + j)
                stage[hd, a, 3 * j:3 * j + 3, :] = code
                scales = jnp.where(lane == 3 * j + sub, scale, scales)
            stage[hd, a, 15:16, :] = jnp.sum(scales, axis=0, keepdims=True)
        sbuf[hd] = stage[hd].astype(BF16)

    for hd in range(NL):
        for j in range(GH):
            g = GH * hd + j
            qstage[hd, 3 * j:3 * j + 3, :] = q_in[:, g * HD:(g + 1) * HD].astype(F32)
    qsend[...] = qstage[...].astype(BF16)

    pl.semaphore_wait(barrier, (NZ - 1) + (NXY - 1) + 1)

    def zcopy(z2, mine, theirs):
        return pltpu.make_async_remote_copy(
            src_ref=sbuf.at[lax.rem(z2, NL)], dst_ref=rbuf.at[mine], send_sem=zs.at[z2], recv_sem=zr.at[theirs],
            device_id=zdev(z2), device_id_type=MESH)

    def wcopy(d):
        z2 = near(-d)
        pos = place(z2, d)
        return pltpu.make_async_remote_copy(
            src_ref=qsend.at[lax.rem(z2, NL)], dst_ref=qrecv.at[pos], send_sem=ws.at[d + 3], recv_sem=wr.at[pos],
            device_id=zdev(z2), device_id_type=MESH)

    def wait_owner(pos):
        pltpu.make_async_remote_copy(
            src_ref=qsend.at[0], dst_ref=qrecv.at[pos], send_sem=ws.at[0], recv_sem=wr.at[pos],
            device_id=zdev(near(1)), device_id_type=MESH).wait_recv()

    for d in REACH:
        wcopy(d).start()

    @pl.loop(0, NZ - 1)
    def _(k):
        zcopy(zfar(k), z, z).start()

    rbuf[z] = sbuf[h]

    own = place(z, 0)
    qrecv[own] = qsend[h]

    col = iota((1, NZ * 16), 1)
    src = jnp.right_shift(col, 4)
    row16 = jnp.bitwise_and(col, 15)
    j_of = third(row16)
    key = ZT * j_of + TOK * src + row16 - 3 * j_of
    key = jnp.where(row16 < 15, key, -1)
    for n in range(GH):
        pmat[n * ZT:(n + 1) * ZT, :] = one_hot(iota((ZT, NZ * 16), 0) + n * ZT == key)
    token = iota((ZT, NZ * 16), 0) - TOK * src
    pmat[GH * ZT:, :] = one_hot((token >= 0) & (token < TOK) & (row16 == 15))
    to_slots = one_hot(iota((SLOTS, NP * 16), 0) == slot_of(iota((SLOTS, NP * 16), 1)))
    to_owners = one_hot(slot_of(iota((NP * 16, SLOTS), 0)) == iota((NP * 16, SLOTS), 1))

    def pcopy(src, dst, xy2, half, theirs, ssem, rsem):
        return pltpu.make_async_remote_copy(
            src_ref=src, dst_ref=dst, send_sem=ssem.at[half, xy2], recv_sem=rsem.at[half, theirs],
            device_id=pdev(xy2), device_id_type=MESH)

    for half in range(2):
        for pos in range(NP * half, NP * half + NP):

            @pl.when(pos != own)
            def _():
                wait_owner(pos)

        qall[half, xy] = jnp.dot(
            to_slots, qrecv[NP * half:NP * half + NP].reshape(NP * 16, HD), preferred_element_type=F32).astype(BF16)

        @pl.loop(0, NXY - 1)
        def _(k):
            pcopy(qall.at[half, xy], qall.at[half, xy], pfar(k), half, xy, qs, qr).start()

    for copy in base_copies:
        copy.wait()
    bf32[...] = bwin[...].astype(F32)

    token_in = iota((ZT, HD), 0)
    lane_of = iota((ZT, HD), 1) - (token_in - 3 * third(token_in))
    ones = jnp.ones((HD, HD), BF16)
    shift = pl.ds(pl.multiple_of(8 * lax.rem(xyc, 2), 8), HT)

    def ccopy(a):
        buf = (kall, vall)[a]
        return pltpu.make_async_remote_copy(
            src_ref=buf.at[core], dst_ref=buf.at[core], send_sem=cs.at[a], recv_sem=cr.at[a],
            device_id=cdev(), device_id_type=MESH)

    @pl.loop(0, NZ - 1)
    def _(k):
        z2 = zfar(NZ - 2 - k)
        zcopy(z2, z, z2).wait_recv()

    def rebuild(a):
        picked = jnp.dot(pmat[...], rbuf[:, a].reshape(NZ * 16, HD), preferred_element_type=F32)
        scales = picked[GH * ZT:]
        by_head = [jnp.where(lane_of == 3 * j, scales, 0.0).astype(BF16) for j in range(GH)]
        steps = jnp.dot(jnp.concatenate(by_head, axis=0), ones, preferred_element_type=F32) / 127.0
        for j in range(GH):
            base = jnp.concatenate(
                [bf32[a, half, shift, j * HD:(j + 1) * HD] for half in range(2)], axis=0)
            rows = slice(j * ZT, (j + 1) * ZT)
            (kall, vall)[a][core, j] = (base + picked[rows] * steps[rows]).astype(BF16)
        ccopy(a).start()

    rebuild(0)
    rebuild(1)
    ccopy(0).wait_recv()

    slot_lane = jnp.bitwise_and(iota((1, QUAD * SLOTS), 1), SLOTS - 1)
    stat_row = iota((8, QUAD * SLOTS), 0)
    last_rows = iota((8, HD), 0) >= 4
    head_slots = NP * TOK

    def weigh(half, first, k):
        for c in range(QUAD):
            tile = first + c

            @pl.when(tile != xy)
            def _():
                pcopy(qall.at[half, tile], qall.at[half, tile], tile, half, tile, qs, qr).wait_recv()

        queries = qall[half, pl.ds(first, QUAD)].reshape(QUAD * SLOTS, HD)
        stacked = lax.dot_general(
            kall[...].reshape(GH * KEYS, HD), queries, NT, preferred_element_type=F32)
        blocks = []
        for c in range(NC):
            block = stacked[(GH * c + GH - 1) * ZT:(GH * c + GH) * ZT]
            for j in range(GH - 2, -1, -1):
                rows = stacked[(GH * c + j) * ZT:(GH * c + j + 1) * ZT]
                block = jnp.where(slot_lane < head_slots * (j + 1), rows, block)
            blocks.append(block)
        scores = jnp.concatenate(blocks, axis=0) * SCALE2
        peak = jnp.max(scores, axis=0, keepdims=True)
        peak_hi = peak.astype(BF16).astype(F32)
        peak_lo = (peak - peak_hi).astype(BF16).astype(F32)
        weights = jnp.exp2(scores - (peak_hi + peak_lo))
        total = jnp.sum(weights, axis=0, keepdims=True)
        total_hi = total.astype(BF16).astype(F32)
        total_lo = total - total_hi
        for c in range(NC):
            for j in range(GH):
                in_head = slot_lane >= head_slots * j
                if j < GH - 1:
                    in_head = in_head & (slot_lane < head_slots * (j + 1))
                n = GH * c + j
                pbuf[k, n * ZT:(n + 1) * ZT, :] = jnp.where(
                    in_head, weights[c * ZT:(c + 1) * ZT], 0.0).astype(BF16)
        stbuf[k] = jnp.where(stat_row == 4, peak_hi, jnp.where(
            stat_row == 5, peak_lo, jnp.where(stat_row == 6, total_hi, total_lo)))

    def mix(half, first, k):
        mixed = jnp.dot(vt[...], pbuf[k], preferred_element_type=F32).T
        for c in range(QUAD):
            part = mixed[c * SLOTS:(c + 1) * SLOTS]
            stat = stbuf[k, :, (c // 2) * HD:(c // 2 + 1) * HD]
            if c % 2:
                stat = pltpu.roll(stat, SLOTS, 1)
            tail = jnp.where(last_rows, stat, part[SLOTS - 8:])
            obuf[half, first + c] = jnp.concatenate([part[:SLOTS - 8], tail], axis=0).astype(BF16)
        for c in range(QUAD):
            tile = first + c

            @pl.when(tile != xy)
            def _():
                pcopy(obuf.at[half, tile], orecv.at[half, xy], tile, half, xy, osm, orm).start()

            @pl.when(tile == xy)
            def _():
                orecv[half, tile] = obuf[half, tile]

    quads = NXY // QUAD

    def quad_at(k):
        turn = (2 * lax.rem(k, 2) - 1) * lax.div(k + 1, 2)
        return QUAD * lax.rem(lax.div(xy, QUAD) + quads // 2 + turn + quads, quads)

    @pl.loop(0, quads // 2)
    def _(k):
        weigh(0, quad_at(k), k)

    ccopy(1).wait_recv()
    eye = one_hot(iota((HD, HD), 0) == iota((HD, HD), 1))
    vt[...] = lax.dot_general(
        eye, vall[...].reshape(GH * KEYS, HD), NT, preferred_element_type=F32).astype(BF16)

    @pl.loop(0, quads // 2)
    def _(k):
        mix(0, quad_at(k), k)

    @pl.loop(quads // 2, quads)
    def _(k):
        weigh(0, quad_at(k), k)
        mix(0, quad_at(k), k)

    @pl.loop(0, quads)
    def _(k):
        weigh(1, quad_at(k), k)

    @pl.loop(0, quads)
    def _(k):
        mix(1, quad_at(k), k)

    def fcopy(pos, theirs):
        return pltpu.make_async_remote_copy(
            src_ref=fbuf.at[pos], dst_ref=frecv.at[h], send_sem=fs.at[pos], recv_sem=fr.at[theirs],
            device_id=zdev(near(owner_at(z, pos))), device_id_type=MESH)

    for half in range(2):

        @pl.loop(1, NXY)
        def _(k):
            xy2 = lax.rem(xy + k, NXY)
            pcopy(obuf.at[half, xy2], orecv.at[half, xy2], xy2, half, xy2, osm, orm).wait_recv()

        stats = [orecv[half, n, SLOTS - 16:SLOTS, :].astype(F32) for n in range(NXY)]
        peaks = [st[12:13] + st[13:14] for st in stats]
        top = peaks[0]
        for n in range(1, NXY):
            top = jnp.maximum(top, peaks[n])
        parts = [jnp.exp2(peaks[n] - top) for n in range(NXY)]
        total = jnp.zeros((1, HD), F32)
        for n in range(NXY):
            total = total + parts[n] * (stats[n][14:15] + stats[n][15:16])
        for n in range(NXY):
            coef[n:n + 1, :] = parts[n] / total
        columns = coef[...].T
        joined = jnp.zeros((SLOTS, HD), F32)
        for n in range(NXY):
            joined = joined + orecv[half, n].astype(F32) * columns[0:SLOTS, n:n + 1]
        owned = jnp.dot(to_owners, joined.astype(BF16), preferred_element_type=F32)
        fbuf[NP * half:NP * half + NP] = owned.astype(BF16).reshape(NP, 16, HD)
        for pos in range(NP * half, NP * half + NP):

            @pl.when(pos != own)
            def _():
                fcopy(pos, h).start()

            @pl.when(pos == own)
            def _():
                frecv[h] = fbuf[pos]

    @pl.loop(0, NZ - 1)
    def _(k):
        zcopy(zfar(k), z, z).wait_send()

    for d in REACH:
        wcopy(d).wait_send()

    for a in range(2):
        ccopy(a).wait_send()

    @pl.loop(1, NXY)
    def _(k):
        xy2 = lax.rem(xy + k, NXY)
        for half in range(2):
            pcopy(qall.at[half, xy], qall.at[half, xy], xy2, half, xy2, qs, qr).wait_send()
            pcopy(obuf.at[half, xy2], orecv.at[half, xy], xy2, half, xy2, osm, orm).wait_send()

    @pl.loop(1, NL)
    def _(k):
        h2 = lax.rem(h + k, NL)
        pltpu.make_async_remote_copy(
            src_ref=fbuf.at[0], dst_ref=frecv.at[h2], send_sem=fs.at[0], recv_sem=fr.at[h2],
            device_id=zdev(near(1)), device_id_type=MESH).wait_recv()

    fstage[...] = frecv[...].astype(F32)
    for hd in range(NL):
        for j in range(GH):
            g = GH * hd + j
            fout[:, g * HD:(g + 1) * HD] = fstage[hd, 3 * j:3 * j + 3, :]
    out_ref[...] = fout[...].astype(BF16)

    for pos in range(NL):

        @pl.when(pos != own)
        def _():
            fcopy(pos, h).wait_send()


def on_device(query, delta_key, delta_value, base_key, base_value):
    vmem = pl.BlockSpec(memory_space=pltpu.VMEM)
    hbm = pl.BlockSpec(memory_space=pl.ANY)
    dma = pltpu.SemaphoreType.DMA
    return pl.pallas_call(
        kernel,
        out_shape=jax.ShapeDtypeStruct(query.shape, BF16),
        in_specs=[hbm] * 5,
        out_specs=vmem,
        scratch_shapes=[
            pltpu.VMEM((NL, 2, 16, HD), F32),
            pltpu.VMEM((NL, 16, HD), F32),
            pltpu.VMEM((NL, 2, 16, HD), BF16),
            pltpu.VMEM((NL, 16, HD), BF16),
            pltpu.VMEM((NZ, 2, 16, HD), BF16),
            pltpu.VMEM((NL, 16, HD), BF16),
            pltpu.VMEM(((GH + 1) * ZT, NZ * 16), BF16),
            pltpu.VMEM((2, 2, 32, GW), BF16),
            pltpu.VMEM((2, 2, 32, GW), F32),
            pltpu.VMEM((NC, GH, ZT, HD), BF16),
            pltpu.VMEM((NC, GH, ZT, HD), BF16),
            pltpu.VMEM((2, NXY, SLOTS, HD), BF16),
            pltpu.VMEM((HD, GH * KEYS), BF16),
            pltpu.VMEM((NXY // QUAD, GH * KEYS, QUAD * SLOTS), BF16),
            pltpu.VMEM((NXY // QUAD, 8, QUAD * SLOTS), F32),
            pltpu.VMEM((2, NXY, SLOTS, HD), BF16),
            pltpu.VMEM((2, NXY, SLOTS, HD), BF16),
            pltpu.VMEM((NXY, HD), F32),
            pltpu.VMEM((NL, 16, HD), BF16),
            pltpu.VMEM((NL, 16, HD), BF16),
            pltpu.VMEM((NL, 16, HD), F32),
            pltpu.VMEM(query.shape, F32),
            pltpu.VMEM(query.shape, BF16),
            pltpu.VMEM(query.shape, F32),
            pltpu.VMEM(query.shape, F32),
            dma((3,)), dma((4,)), dma((NZ,)), dma((NZ,)), dma((NL,)), dma((NL,)), dma((2,)), dma((2,)),
            dma((2, NXY)), dma((2, NXY)), dma((2, NXY)), dma((2, NXY)), dma((NL,)), dma((NL,)),
        ],
        compiler_params=pltpu.CompilerParams(
            collective_id=0, has_side_effects=True, vmem_limit_bytes=60 * 1024 * 1024),
    )(query, delta_key, delta_value, base_key, base_value)


def solution(mesh):
    rows = P(("patch", "head"), None)
    cols = P(None, "head")
    return jax.shard_map(
        on_device, mesh=mesh, in_specs=(rows, rows, rows, cols, cols), out_specs=rows, check_vma=False)
```

```python
import math

import jax
import jax.numpy as jnp
from jax import lax
from jax.experimental import pallas as pl
from jax.experimental.pallas import tpu as pltpu
from jax.sharding import PartitionSpec as P

MESH = pl.DeviceIdType.MESH
F32 = jnp.float32
BF16 = jnp.bfloat16

HD = 128
NX, NY, NC = 4, 4, 2
NL = 8
NZ = 2 * NL
GH = 5
GW = GH * HD
TOK = 3
ZT = TOK * NZ
HT = TOK * NL
NXY = NX * NY
PLANE = NXY * NC
KEYS = NC * ZT
NP = NL // 2
SLOTS = 64
QUAD = 4
REACH = (4, -3, 3, -2, 2, -1, 1)
SCALE2 = math.log2(math.e) / math.sqrt(HD)

NT = (((1,), (1,)), ((), ()))


def iota(shape, dim):
    return lax.broadcasted_iota(jnp.int32, shape, dim)


def one_hot(cond):
    return jnp.where(cond, 1.0, 0.0).astype(BF16)


def third(n):
    return jnp.right_shift(n * 43, 7)


def slot_of(r):
    rr = jnp.bitwise_and(r, 15)
    j = third(rr)
    slot = NP * TOK * j + TOK * jnp.right_shift(r, 4) + rr - 3 * j
    return jnp.where(rr < 15, slot, -1)


def place(home, d):
    return lax.rem(d + 3 + jnp.minimum(lax.rem(home + 5, NZ), NL), NL)


def owner_at(home, pos):
    return lax.rem(pos - jnp.minimum(lax.rem(home + 5, NZ), NL) + NL, NL) - 3


def kernel(
    q_ref, dk_ref, dv_ref, bk_ref, bv_ref, out_ref,
    stage, qstage, sbuf, qsend, rbuf, qrecv, pmat, bwin, bf32,
    kall, vall, qall, vt, pbuf, stbuf, obuf, orecv, coef, fbuf, frecv, fstage, fout, q_in, dk_in, dv_in,
    isem, bsem, zs, zr, ws, wr, cs, cr, qs, qr, osm, orm, fs, fr,
):
    p = lax.axis_index("patch")
    h = lax.axis_index("head")
    zh = lax.div(p, PLANE)
    xyc = lax.rem(p, PLANE)
    xy = lax.div(xyc, NC)
    core = lax.rem(xyc, NC)
    z = zh * NL + h

    def zdev(z2):
        return (lax.div(z2, NL) * PLANE + xyc, lax.rem(z2, NL))

    def pfar(k):
        turn_x = lax.div(k, NY)
        turn_y = lax.rem(k, NY)
        x2 = lax.rem(lax.div(xy, NY) + NX // 2 + (2 * lax.rem(turn_x, 2) - 1) * lax.div(turn_x + 1, 2) + NX, NX)
        y2 = lax.rem(lax.rem(xy, NY) + NY // 2 + (2 * lax.rem(turn_y, 2) - 1) * lax.div(turn_y + 1, 2) + NY, NY)
        return x2 * NY + y2

    def pdev(xy2):
        return (zh * PLANE + xy2 * NC + core, h)

    def zfar(k):
        half = lax.div(k + 1, 2)
        return lax.rem(z + NL + (2 * lax.rem(k, 2) - 1) * half + NZ, NZ)

    def near(d):
        return lax.rem(z + d + NZ, NZ)

    def cdev():
        return (zh * PLANE + xy * NC + 1 - core, h)

    barrier = pltpu.get_barrier_semaphore()

    @pl.loop(0, NZ - 1)
    def _(k):
        pl.semaphore_signal(barrier, inc=1, device_id=zdev(zfar(k)), device_id_type=MESH)

    @pl.loop(1, NXY)
    def _(k):
        pl.semaphore_signal(barrier, inc=1, device_id=pdev(lax.rem(xy + k, NXY)), device_id_type=MESH)

    pl.semaphore_signal(barrier, inc=1, device_id=cdev(), device_id_type=MESH)

    base_copies = []
    for a, ref in enumerate((bk_ref, bv_ref)):
        for half in range(2):
            row0 = pl.multiple_of(lax.div(HT * (xyc + half * PLANE), 16) * 16, 16)
            base_copies.append(pltpu.make_async_copy(
                ref.at[pl.ds(row0, 32)], bwin.at[a, half], bsem.at[2 * a + half]))
    in_copies = [
        pltpu.make_async_copy(src, dst, isem.at[n])
        for n, (src, dst) in enumerate(((dk_ref, dk_in), (dv_ref, dv_in), (q_ref, q_in)))]
    for copy in in_copies:
        copy.start()
    for copy in base_copies:
        copy.start()

    lane = iota((TOK, HD), 1)
    sub = iota((TOK, HD), 0)
    for copy in in_copies:
        copy.wait()
    qstage[:, 15:16, :] = jnp.zeros((NL, 1, HD), F32)

    def encode(ref, g):
        block = ref[:, g * HD:(g + 1) * HD]
        scale = (jnp.max(jnp.abs(block), axis=1, keepdims=True) + 1e-06).astype(BF16).astype(F32)
        levels = jnp.floor(127.0 * block / scale + 0.5)
        return jnp.clip(levels, -127.0, 127.0), scale

    for hd in range(NL):
        for a, ref in enumerate((dk_in, dv_in)):
            scales = jnp.zeros((TOK, HD), F32)
            for j in range(GH):
                code, scale = encode(ref, GH * hd + j)
                stage[hd, a, 3 * j:3 * j + 3, :] = code
                scales = jnp.where(lane == 3 * j + sub, scale, scales)
            stage[hd, a, 15:16, :] = jnp.sum(scales, axis=0, keepdims=True)
        sbuf[hd] = stage[hd].astype(BF16)

    for hd in range(NL):
        for j in range(GH):
            g = GH * hd + j
            qstage[hd, 3 * j:3 * j + 3, :] = q_in[:, g * HD:(g + 1) * HD].astype(F32)
    qsend[...] = qstage[...].astype(BF16)

    pl.semaphore_wait(barrier, (NZ - 1) + (NXY - 1) + 1)

    def zcopy(z2, mine, theirs):
        return pltpu.make_async_remote_copy(
            src_ref=sbuf.at[lax.rem(z2, NL)], dst_ref=rbuf.at[mine], send_sem=zs.at[z2], recv_sem=zr.at[theirs],
            device_id=zdev(z2), device_id_type=MESH)

    def wcopy(d):
        z2 = near(-d)
        pos = place(z2, d)
        return pltpu.make_async_remote_copy(
            src_ref=qsend.at[lax.rem(z2, NL)], dst_ref=qrecv.at[pos], send_sem=ws.at[d + 3], recv_sem=wr.at[pos],
            device_id=zdev(z2), device_id_type=MESH)

    def wait_owner(pos):
        pltpu.make_async_remote_copy(
            src_ref=qsend.at[0], dst_ref=qrecv.at[pos], send_sem=ws.at[0], recv_sem=wr.at[pos],
            device_id=zdev(near(1)), device_id_type=MESH).wait_recv()

    for d in REACH:
        wcopy(d).start()

    @pl.loop(0, NZ - 1)
    def _(k):
        zcopy(zfar(k), z, z).start()

    rbuf[z] = sbuf[h]

    own = place(z, 0)
    qrecv[own] = qsend[h]

    col = iota((1, NZ * 16), 1)
    src = jnp.right_shift(col, 4)
    row16 = jnp.bitwise_and(col, 15)
    j_of = third(row16)
    key = ZT * j_of + TOK * src + row16 - 3 * j_of
    key = jnp.where(row16 < 15, key, -1)
    for n in range(GH):
        pmat[n * ZT:(n + 1) * ZT, :] = one_hot(iota((ZT, NZ * 16), 0) + n * ZT == key)
    token = iota((ZT, NZ * 16), 0) - TOK * src
    pmat[GH * ZT:, :] = one_hot((token >= 0) & (token < TOK) & (row16 == 15))
    to_slots = one_hot(iota((SLOTS, NP * 16), 0) == slot_of(iota((SLOTS, NP * 16), 1)))
    to_owners = one_hot(slot_of(iota((NP * 16, SLOTS), 0)) == iota((NP * 16, SLOTS), 1))

    def pcopy(src, dst, xy2, half, theirs, ssem, rsem):
        return pltpu.make_async_remote_copy(
            src_ref=src, dst_ref=dst, send_sem=ssem.at[half, xy2], recv_sem=rsem.at[half, theirs],
            device_id=pdev(xy2), device_id_type=MESH)

    for half in range(2):
        for pos in range(NP * half, NP * half + NP):

            @pl.when(pos != own)
            def _():
                wait_owner(pos)

        qall[half, xy] = jnp.dot(
            to_slots, qrecv[NP * half:NP * half + NP].reshape(NP * 16, HD), preferred_element_type=F32).astype(BF16)

        @pl.loop(0, NXY - 1)
        def _(k):
            pcopy(qall.at[half, xy], qall.at[half, xy], pfar(k), half, xy, qs, qr).start()

    for copy in base_copies:
        copy.wait()
    bf32[...] = bwin[...].astype(F32)

    token_in = iota((ZT, HD), 0)
    lane_of = iota((ZT, HD), 1) - (token_in - 3 * third(token_in))
    ones = jnp.ones((HD, HD), BF16)
    shift = pl.ds(pl.multiple_of(8 * lax.rem(xyc, 2), 8), HT)

    def ccopy(a):
        buf = (kall, vall)[a]
        return pltpu.make_async_remote_copy(
            src_ref=buf.at[core], dst_ref=buf.at[core], send_sem=cs.at[a], recv_sem=cr.at[a],
            device_id=cdev(), device_id_type=MESH)

    @pl.loop(0, NZ - 1)
    def _(k):
        z2 = zfar(NZ - 2 - k)
        zcopy(z2, z, z2).wait_recv()

    def rebuild(a):
        picked = jnp.dot(pmat[...], rbuf[:, a].reshape(NZ * 16, HD), preferred_element_type=F32)
        scales = picked[GH * ZT:]
        by_head = [jnp.where(lane_of == 3 * j, scales, 0.0).astype(BF16) for j in range(GH)]
        steps = jnp.dot(jnp.concatenate(by_head, axis=0), ones, preferred_element_type=F32) / 127.0
        for j in range(GH):
            base = jnp.concatenate(
                [bf32[a, half, shift, j * HD:(j + 1) * HD] for half in range(2)], axis=0)
            rows = slice(j * ZT, (j + 1) * ZT)
            (kall, vall)[a][core, j] = (base + picked[rows] * steps[rows]).astype(BF16)
        ccopy(a).start()

    rebuild(0)
    rebuild(1)
    ccopy(0).wait_recv()

    slot_lane = jnp.bitwise_and(iota((1, QUAD * SLOTS), 1), SLOTS - 1)
    stat_row = iota((8, QUAD * SLOTS), 0)
    last_rows = iota((8, HD), 0) >= 4
    head_slots = NP * TOK

    def weigh(half, first, k):
        for c in range(QUAD):
            tile = first + c

            @pl.when(tile != xy)
            def _():
                pcopy(qall.at[half, tile], qall.at[half, tile], tile, half, tile, qs, qr).wait_recv()

        queries = qall[half, pl.ds(first, QUAD)].reshape(QUAD * SLOTS, HD)
        stacked = lax.dot_general(
            kall[...].reshape(GH * KEYS, HD), queries, NT, preferred_element_type=F32)
        blocks = []
        for c in range(NC):
            block = stacked[(GH * c + GH - 1) * ZT:(GH * c + GH) * ZT]
            for j in range(GH - 2, -1, -1):
                rows = stacked[(GH * c + j) * ZT:(GH * c + j + 1) * ZT]
                block = jnp.where(slot_lane < head_slots * (j + 1), rows, block)
            blocks.append(block)
        scores = jnp.concatenate(blocks, axis=0) * SCALE2
        peak = jnp.max(scores, axis=0, keepdims=True)
        peak_hi = peak.astype(BF16).astype(F32)
        peak_lo = (peak - peak_hi).astype(BF16).astype(F32)
        weights = jnp.exp2(scores - (peak_hi + peak_lo))
        total = jnp.sum(weights, axis=0, keepdims=True)
        total_hi = total.astype(BF16).astype(F32)
        total_lo = total - total_hi
        for c in range(NC):
            for j in range(GH):
                in_head = slot_lane >= head_slots * j
                if j < GH - 1:
                    in_head = in_head & (slot_lane < head_slots * (j + 1))
                n = GH * c + j
                pbuf[k, n * ZT:(n + 1) * ZT, :] = jnp.where(
                    in_head, weights[c * ZT:(c + 1) * ZT], 0.0).astype(BF16)
        stbuf[k] = jnp.where(stat_row == 4, peak_hi, jnp.where(
            stat_row == 5, peak_lo, jnp.where(stat_row == 6, total_hi, total_lo)))

    def mix(half, first, k):
        mixed = jnp.dot(vt[...], pbuf[k], preferred_element_type=F32).T
        for c in range(QUAD):
            part = mixed[c * SLOTS:(c + 1) * SLOTS]
            stat = stbuf[k, :, (c // 2) * HD:(c // 2 + 1) * HD]
            if c % 2:
                stat = pltpu.roll(stat, SLOTS, 1)
            tail = jnp.where(last_rows, stat, part[SLOTS - 8:])
            obuf[half, first + c] = jnp.concatenate([part[:SLOTS - 8], tail], axis=0).astype(BF16)
        for c in range(QUAD):
            tile = first + lax.rem(xy + (2, 1, 3, 0)[c], QUAD)

            @pl.when(tile != xy)
            def _():
                pcopy(obuf.at[half, tile], orecv.at[half, xy], tile, half, xy, osm, orm).start()

            @pl.when(tile == xy)
            def _():
                orecv[half, tile] = obuf[half, tile]

    quads = NXY // QUAD

    def quad_at(k):
        turn = (2 * lax.rem(k, 2) - 1) * lax.div(k + 1, 2)
        return QUAD * lax.rem(lax.div(xy, QUAD) + quads // 2 + turn + quads, quads)

    @pl.loop(0, quads // 2)
    def _(k):
        weigh(0, quad_at(k), k)

    ccopy(1).wait_recv()
    eye = one_hot(iota((HD, HD), 0) == iota((HD, HD), 1))
    vt[...] = lax.dot_general(
        eye, vall[...].reshape(GH * KEYS, HD), NT, preferred_element_type=F32).astype(BF16)

    @pl.loop(0, quads // 2)
    def _(k):
        mix(0, quad_at(k), k)

    @pl.loop(quads // 2, quads)
    def _(k):
        weigh(0, quad_at(k), k)
        mix(0, quad_at(k), k)

    @pl.loop(0, quads)
    def _(k):
        weigh(1, quad_at(k), k)

    @pl.loop(0, quads)
    def _(k):
        mix(1, quad_at(k), k)

    def fcopy(pos, theirs):
        return pltpu.make_async_remote_copy(
            src_ref=fbuf.at[pos], dst_ref=frecv.at[h], send_sem=fs.at[pos], recv_sem=fr.at[theirs],
            device_id=zdev(near(owner_at(z, pos))), device_id_type=MESH)

    for half in range(2):

        @pl.loop(1, NXY)
        def _(k):
            xy2 = lax.rem(xy + k, NXY)
            pcopy(obuf.at[half, xy2], orecv.at[half, xy2], xy2, half, xy2, osm, orm).wait_recv()

        stats = [orecv[half, n, SLOTS - 16:SLOTS, :].astype(F32) for n in range(NXY)]
        peaks = [st[12:13] + st[13:14] for st in stats]
        top = peaks[0]
        for n in range(1, NXY):
            top = jnp.maximum(top, peaks[n])
        parts = [jnp.exp2(peaks[n] - top) for n in range(NXY)]
        total = jnp.zeros((1, HD), F32)
        for n in range(NXY):
            total = total + parts[n] * (stats[n][14:15] + stats[n][15:16])
        for n in range(NXY):
            coef[n:n + 1, :] = parts[n] / total
        columns = coef[...].T
        joined = jnp.zeros((SLOTS, HD), F32)
        for n in range(NXY):
            joined = joined + orecv[half, n].astype(F32) * columns[0:SLOTS, n:n + 1]
        owned = jnp.dot(to_owners, joined.astype(BF16), preferred_element_type=F32)
        fbuf[NP * half:NP * half + NP] = owned.astype(BF16).reshape(NP, 16, HD)
        for pos in range(NP * half, NP * half + NP):

            @pl.when(pos != own)
            def _():
                fcopy(pos, h).start()

            @pl.when(pos == own)
            def _():
                frecv[h] = fbuf[pos]

    @pl.loop(0, NZ - 1)
    def _(k):
        zcopy(zfar(k), z, z).wait_send()

    for d in REACH:
        wcopy(d).wait_send()

    for a in range(2):
        ccopy(a).wait_send()

    @pl.loop(1, NXY)
    def _(k):
        xy2 = lax.rem(xy + k, NXY)
        for half in range(2):
            pcopy(qall.at[half, xy], qall.at[half, xy], xy2, half, xy2, qs, qr).wait_send()
            pcopy(obuf.at[half, xy2], orecv.at[half, xy], xy2, half, xy2, osm, orm).wait_send()

    @pl.loop(1, NL)
    def _(k):
        h2 = lax.rem(h + k, NL)
        pltpu.make_async_remote_copy(
            src_ref=fbuf.at[0], dst_ref=frecv.at[h2], send_sem=fs.at[0], recv_sem=fr.at[h2],
            device_id=zdev(near(1)), device_id_type=MESH).wait_recv()

    fstage[...] = frecv[...].astype(F32)
    for hd in range(NL):
        for j in range(GH):
            g = GH * hd + j
            fout[:, g * HD:(g + 1) * HD] = fstage[hd, 3 * j:3 * j + 3, :]
    out_ref[...] = fout[...].astype(BF16)

    for pos in range(NL):

        @pl.when(pos != own)
        def _():
            fcopy(pos, h).wait_send()


def on_device(query, delta_key, delta_value, base_key, base_value):
    vmem = pl.BlockSpec(memory_space=pltpu.VMEM)
    hbm = pl.BlockSpec(memory_space=pl.ANY)
    dma = pltpu.SemaphoreType.DMA
    return pl.pallas_call(
        kernel,
        out_shape=jax.ShapeDtypeStruct(query.shape, BF16),
        in_specs=[hbm] * 5,
        out_specs=vmem,
        scratch_shapes=[
            pltpu.VMEM((NL, 2, 16, HD), F32),
            pltpu.VMEM((NL, 16, HD), F32),
            pltpu.VMEM((NL, 2, 16, HD), BF16),
            pltpu.VMEM((NL, 16, HD), BF16),
            pltpu.VMEM((NZ, 2, 16, HD), BF16),
            pltpu.VMEM((NL, 16, HD), BF16),
            pltpu.VMEM(((GH + 1) * ZT, NZ * 16), BF16),
            pltpu.VMEM((2, 2, 32, GW), BF16),
            pltpu.VMEM((2, 2, 32, GW), F32),
            pltpu.VMEM((NC, GH, ZT, HD), BF16),
            pltpu.VMEM((NC, GH, ZT, HD), BF16),
            pltpu.VMEM((2, NXY, SLOTS, HD), BF16),
            pltpu.VMEM((HD, GH * KEYS), BF16),
            pltpu.VMEM((NXY // QUAD, GH * KEYS, QUAD * SLOTS), BF16),
            pltpu.VMEM((NXY // QUAD, 8, QUAD * SLOTS), F32),
            pltpu.VMEM((2, NXY, SLOTS, HD), BF16),
            pltpu.VMEM((2, NXY, SLOTS, HD), BF16),
            pltpu.VMEM((NXY, HD), F32),
            pltpu.VMEM((NL, 16, HD), BF16),
            pltpu.VMEM((NL, 16, HD), BF16),
            pltpu.VMEM((NL, 16, HD), F32),
            pltpu.VMEM(query.shape, F32),
            pltpu.VMEM(query.shape, BF16),
            pltpu.VMEM(query.shape, F32),
            pltpu.VMEM(query.shape, F32),
            dma((3,)), dma((4,)), dma((NZ,)), dma((NZ,)), dma((NL,)), dma((NL,)), dma((2,)), dma((2,)),
            dma((2, NXY)), dma((2, NXY)), dma((2, NXY)), dma((2, NXY)), dma((NL,)), dma((NL,)),
        ],
        compiler_params=pltpu.CompilerParams(
            collective_id=0, has_side_effects=True, vmem_limit_bytes=60 * 1024 * 1024),
    )(query, delta_key, delta_value, base_key, base_value)


def solution(mesh):
    rows = P(("patch", "head"), None)
    cols = P(None, "head")
    return jax.shard_map(
        on_device, mesh=mesh, in_specs=(rows, rows, rows, cols, cols), out_specs=rows, check_vma=False)
```

```python
import math

import jax
import jax.numpy as jnp
from jax import lax
from jax.experimental import pallas as pl
from jax.experimental.pallas import tpu as pltpu
from jax.sharding import PartitionSpec as P

MESH = pl.DeviceIdType.MESH
F32 = jnp.float32
BF16 = jnp.bfloat16

HD = 128
NX, NY, NC = 4, 4, 2
NL = 8
NZ = 2 * NL
GH = 5
GW = GH * HD
TOK = 3
ZT = TOK * NZ
HT = TOK * NL
NXY = NX * NY
PLANE = NXY * NC
KEYS = NC * ZT
NP = NL // 2
SLOTS = 64
QUAD = 4
REACH = (4, -3, 3, -2, 2, -1, 1)
SCALE2 = math.log2(math.e) / math.sqrt(HD)

NT = (((1,), (1,)), ((), ()))


def iota(shape, dim):
    return lax.broadcasted_iota(jnp.int32, shape, dim)


def one_hot(cond):
    return jnp.where(cond, 1.0, 0.0).astype(BF16)


def third(n):
    return jnp.right_shift(n * 43, 7)


def slot_of(r):
    rr = jnp.bitwise_and(r, 15)
    j = third(rr)
    slot = NP * TOK * j + TOK * jnp.right_shift(r, 4) + rr - 3 * j
    return jnp.where(rr < 15, slot, -1)


def place(home, d):
    return lax.rem(d + 3 + jnp.minimum(lax.rem(home + 5, NZ), NL), NL)


def owner_at(home, pos):
    return lax.rem(pos - jnp.minimum(lax.rem(home + 5, NZ), NL) + NL, NL) - 3


def kernel(
    q_ref, dk_ref, dv_ref, bk_ref, bv_ref, out_ref,
    stage, qstage, sbuf, qsend, rbuf, qrecv, pmat, bwin, bf32,
    kall, vall, qall, vt, pbuf, stbuf, obuf, orecv, coef, fbuf, frecv, fstage, fout, q_in, dk_in, dv_in,
    isem, bsem, zs, zr, ws, wr, cs, cr, qs, qr, osm, orm, fs, fr,
):
    p = lax.axis_index("patch")
    h = lax.axis_index("head")
    zh = lax.div(p, PLANE)
    xyc = lax.rem(p, PLANE)
    xy = lax.div(xyc, NC)
    core = lax.rem(xyc, NC)
    z = zh * NL + h

    def zdev(z2):
        return (lax.div(z2, NL) * PLANE + xyc, lax.rem(z2, NL))

    def pfar(k):
        turn_x = lax.div(k, NY)
        turn_y = lax.rem(k, NY)
        x2 = lax.rem(lax.div(xy, NY) + NX // 2 + (2 * lax.rem(turn_x, 2) - 1) * lax.div(turn_x + 1, 2) + NX, NX)
        y2 = lax.rem(lax.rem(xy, NY) + NY // 2 + (2 * lax.rem(turn_y, 2) - 1) * lax.div(turn_y + 1, 2) + NY, NY)
        return x2 * NY + y2

    def pdev(xy2):
        return (zh * PLANE + xy2 * NC + core, h)

    def zfar(k):
        half = lax.div(k + 1, 2)
        return lax.rem(z + NL + (2 * lax.rem(k, 2) - 1) * half + NZ, NZ)

    def near(d):
        return lax.rem(z + d + NZ, NZ)

    def cdev():
        return (zh * PLANE + xy * NC + 1 - core, h)

    barrier = pltpu.get_barrier_semaphore()

    @pl.loop(0, NZ - 1)
    def _(k):
        pl.semaphore_signal(barrier, inc=1, device_id=zdev(zfar(k)), device_id_type=MESH)

    @pl.loop(1, NXY)
    def _(k):
        pl.semaphore_signal(barrier, inc=1, device_id=pdev(lax.rem(xy + k, NXY)), device_id_type=MESH)

    pl.semaphore_signal(barrier, inc=1, device_id=cdev(), device_id_type=MESH)

    base_copies = []
    for a, ref in enumerate((bk_ref, bv_ref)):
        for half in range(2):
            row0 = pl.multiple_of(lax.div(HT * (xyc + half * PLANE), 16) * 16, 16)
            base_copies.append(pltpu.make_async_copy(
                ref.at[pl.ds(row0, 32)], bwin.at[a, half], bsem.at[2 * a + half]))
    in_copies = [
        pltpu.make_async_copy(src, dst, isem.at[n])
        for n, (src, dst) in enumerate(((dk_ref, dk_in), (dv_ref, dv_in), (q_ref, q_in)))]
    for copy in in_copies:
        copy.start()
    for copy in base_copies:
        copy.start()

    lane = iota((TOK, HD), 1)
    sub = iota((TOK, HD), 0)
    for copy in in_copies:
        copy.wait()
    qstage[:, 15:16, :] = jnp.zeros((NL, 1, HD), F32)

    def encode(ref, g):
        block = ref[:, g * HD:(g + 1) * HD]
        scale = (jnp.max(jnp.abs(block), axis=1, keepdims=True) + 1e-06).astype(BF16).astype(F32)
        levels = jnp.floor(127.0 * block / scale + 0.5)
        return jnp.clip(levels, -127.0, 127.0), scale

    for hd in range(NL):
        for a, ref in enumerate((dk_in, dv_in)):
            scales = jnp.zeros((TOK, HD), F32)
            for j in range(GH):
                code, scale = encode(ref, GH * hd + j)
                stage[hd, a, 3 * j:3 * j + 3, :] = code
                scales = jnp.where(lane == 3 * j + sub, scale, scales)
            stage[hd, a, 15:16, :] = jnp.sum(scales, axis=0, keepdims=True)
        sbuf[hd] = stage[hd].astype(BF16)

    for hd in range(NL):
        for j in range(GH):
            g = GH * hd + j
            qstage[hd, 3 * j:3 * j + 3, :] = q_in[:, g * HD:(g + 1) * HD].astype(F32)
    qsend[...] = qstage[...].astype(BF16)

    pl.semaphore_wait(barrier, (NZ - 1) + (NXY - 1) + 1)

    def zcopy(z2, mine, theirs):
        return pltpu.make_async_remote_copy(
            src_ref=sbuf.at[lax.rem(z2, NL)], dst_ref=rbuf.at[mine], send_sem=zs.at[z2], recv_sem=zr.at[theirs],
            device_id=zdev(z2), device_id_type=MESH)

    def wcopy(d):
        z2 = near(-d)
        pos = place(z2, d)
        return pltpu.make_async_remote_copy(
            src_ref=qsend.at[lax.rem(z2, NL)], dst_ref=qrecv.at[pos], send_sem=ws.at[d + 3], recv_sem=wr.at[pos],
            device_id=zdev(z2), device_id_type=MESH)

    def wait_owner(pos):
        pltpu.make_async_remote_copy(
            src_ref=qsend.at[0], dst_ref=qrecv.at[pos], send_sem=ws.at[0], recv_sem=wr.at[pos],
            device_id=zdev(near(1)), device_id_type=MESH).wait_recv()

    for d in REACH:
        wcopy(d).start()

    @pl.loop(0, NZ - 1)
    def _(k):
        zcopy(zfar(k), z, z).start()

    rbuf[z] = sbuf[h]

    own = place(z, 0)
    qrecv[own] = qsend[h]

    col = iota((1, NZ * 16), 1)
    src = jnp.right_shift(col, 4)
    row16 = jnp.bitwise_and(col, 15)
    j_of = third(row16)
    key = ZT * j_of + TOK * src + row16 - 3 * j_of
    key = jnp.where(row16 < 15, key, -1)
    for n in range(GH):
        pmat[n * ZT:(n + 1) * ZT, :] = one_hot(iota((ZT, NZ * 16), 0) + n * ZT == key)
    token = iota((ZT, NZ * 16), 0) - TOK * src
    pmat[GH * ZT:, :] = one_hot((token >= 0) & (token < TOK) & (row16 == 15))
    to_slots = one_hot(iota((SLOTS, NP * 16), 0) == slot_of(iota((SLOTS, NP * 16), 1)))
    to_owners = one_hot(slot_of(iota((NP * 16, SLOTS), 0)) == iota((NP * 16, SLOTS), 1))

    def pcopy(src, dst, xy2, half, theirs, ssem, rsem):
        return pltpu.make_async_remote_copy(
            src_ref=src, dst_ref=dst, send_sem=ssem.at[half, xy2], recv_sem=rsem.at[half, theirs],
            device_id=pdev(xy2), device_id_type=MESH)

    for half in range(2):
        for pos in range(NP * half, NP * half + NP):

            @pl.when(pos != own)
            def _():
                wait_owner(pos)

        qall[half, xy] = jnp.dot(
            to_slots, qrecv[NP * half:NP * half + NP].reshape(NP * 16, HD), preferred_element_type=F32).astype(BF16)

        @pl.loop(0, NXY - 1)
        def _(k):
            pcopy(qall.at[half, xy], qall.at[half, xy], pfar(k), half, xy, qs, qr).start()

    for copy in base_copies:
        copy.wait()
    bf32[...] = bwin[...].astype(F32)

    token_in = iota((ZT, HD), 0)
    lane_of = iota((ZT, HD), 1) - (token_in - 3 * third(token_in))
    ones = jnp.ones((HD, HD), BF16)
    shift = pl.ds(pl.multiple_of(8 * lax.rem(xyc, 2), 8), HT)

    def ccopy(a):
        buf = (kall, vall)[a]
        return pltpu.make_async_remote_copy(
            src_ref=buf.at[core], dst_ref=buf.at[core], send_sem=cs.at[a], recv_sem=cr.at[a],
            device_id=cdev(), device_id_type=MESH)

    @pl.loop(0, NZ - 1)
    def _(k):
        z2 = zfar(NZ - 2 - k)
        zcopy(z2, z, z2).wait_recv()

    def rebuild(a):
        picked = jnp.dot(pmat[...], rbuf[:, a].reshape(NZ * 16, HD), preferred_element_type=F32)
        scales = picked[GH * ZT:]
        by_head = [jnp.where(lane_of == 3 * j, scales, 0.0).astype(BF16) for j in range(GH)]
        steps = jnp.dot(jnp.concatenate(by_head, axis=0), ones, preferred_element_type=F32) / 127.0
        for j in range(GH):
            base = jnp.concatenate(
                [bf32[a, half, shift, j * HD:(j + 1) * HD] for half in range(2)], axis=0)
            rows = slice(j * ZT, (j + 1) * ZT)
            (kall, vall)[a][core, j] = (base + picked[rows] * steps[rows]).astype(BF16)
        ccopy(a).start()

    rebuild(0)
    rebuild(1)
    ccopy(0).wait_recv()

    slot_lane = jnp.bitwise_and(iota((1, QUAD * SLOTS), 1), SLOTS - 1)
    stat_row = iota((8, QUAD * SLOTS), 0)
    last_rows = iota((8, HD), 0) >= 4
    head_slots = NP * TOK

    def weigh(half, first, k):
        for c in range(QUAD):
            tile = first + c

            @pl.when(tile != xy)
            def _():
                pcopy(qall.at[half, tile], qall.at[half, tile], tile, half, tile, qs, qr).wait_recv()

        queries = qall[half, pl.ds(first, QUAD)].reshape(QUAD * SLOTS, HD)
        stacked = lax.dot_general(
            kall[...].reshape(GH * KEYS, HD), queries, NT, preferred_element_type=F32)
        blocks = []
        for c in range(NC):
            block = stacked[(GH * c + GH - 1) * ZT:(GH * c + GH) * ZT]
            for j in range(GH - 2, -1, -1):
                rows = stacked[(GH * c + j) * ZT:(GH * c + j + 1) * ZT]
                block = jnp.where(slot_lane < head_slots * (j + 1), rows, block)
            blocks.append(block)
        scores = jnp.concatenate(blocks, axis=0) * SCALE2
        peak = jnp.max(scores, axis=0, keepdims=True)
        peak_hi = peak.astype(BF16).astype(F32)
        peak_lo = (peak - peak_hi).astype(BF16).astype(F32)
        weights = jnp.exp2(scores - (peak_hi + peak_lo))
        total = jnp.sum(weights, axis=0, keepdims=True)
        total_hi = total.astype(BF16).astype(F32)
        total_lo = total - total_hi
        for c in range(NC):
            for j in range(GH):
                in_head = slot_lane >= head_slots * j
                if j < GH - 1:
                    in_head = in_head & (slot_lane < head_slots * (j + 1))
                n = GH * c + j
                pbuf[k, n * ZT:(n + 1) * ZT, :] = jnp.where(
                    in_head, weights[c * ZT:(c + 1) * ZT], 0.0).astype(BF16)
        stbuf[k] = jnp.where(stat_row == 4, peak_hi, jnp.where(
            stat_row == 5, peak_lo, jnp.where(stat_row == 6, total_hi, total_lo)))

    def mix(half, first, k):
        mixed = jnp.dot(vt[...], pbuf[k], preferred_element_type=F32).T
        for c in range(QUAD):
            part = mixed[c * SLOTS:(c + 1) * SLOTS]
            stat = stbuf[k, :, (c // 2) * HD:(c // 2 + 1) * HD]
            if c % 2:
                stat = pltpu.roll(stat, SLOTS, 1)
            tail = jnp.where(last_rows, stat, part[SLOTS - 8:])
            obuf[half, first + c] = jnp.concatenate([part[:SLOTS - 8], tail], axis=0).astype(BF16)
        for c in range(QUAD):
            tile = first + lax.rem(xy + (2, 1, 3, 0)[c], QUAD)

            @pl.when(tile != xy)
            def _():
                pcopy(obuf.at[half, tile], orecv.at[half, xy], tile, half, xy, osm, orm).start()

            @pl.when(tile == xy)
            def _():
                orecv[half, tile] = obuf[half, tile]

    quads = NXY // QUAD

    def quad_at(k):
        turn = (2 * lax.rem(k, 2) - 1) * lax.div(k + 1, 2)
        return QUAD * lax.rem(lax.div(xy, QUAD) + quads // 2 + turn + quads, quads)

    @pl.loop(0, 3)
    def _(k):
        weigh(0, quad_at(k), k)

    ccopy(1).wait_recv()
    eye = one_hot(iota((HD, HD), 0) == iota((HD, HD), 1))
    vt[...] = lax.dot_general(
        eye, vall[...].reshape(GH * KEYS, HD), NT, preferred_element_type=F32).astype(BF16)

    @pl.loop(0, 3)
    def _(k):
        mix(0, quad_at(k), k)

    @pl.loop(3, quads)
    def _(k):
        weigh(0, quad_at(k), k)
        mix(0, quad_at(k), k)

    @pl.loop(0, quads)
    def _(k):
        weigh(1, quad_at(k), k)

    @pl.loop(0, quads)
    def _(k):
        mix(1, quad_at(k), k)

    def fcopy(pos, theirs):
        return pltpu.make_async_remote_copy(
            src_ref=fbuf.at[pos], dst_ref=frecv.at[h], send_sem=fs.at[pos], recv_sem=fr.at[theirs],
            device_id=zdev(near(owner_at(z, pos))), device_id_type=MESH)

    for half in range(2):

        @pl.loop(1, NXY)
        def _(k):
            xy2 = lax.rem(xy + k, NXY)
            pcopy(obuf.at[half, xy2], orecv.at[half, xy2], xy2, half, xy2, osm, orm).wait_recv()

        stats = [orecv[half, n, SLOTS - 16:SLOTS, :].astype(F32) for n in range(NXY)]
        peaks = [st[12:13] + st[13:14] for st in stats]
        top = peaks[0]
        for n in range(1, NXY):
            top = jnp.maximum(top, peaks[n])
        parts = [jnp.exp2(peaks[n] - top) for n in range(NXY)]
        total = jnp.zeros((1, HD), F32)
        for n in range(NXY):
            total = total + parts[n] * (stats[n][14:15] + stats[n][15:16])
        for n in range(NXY):
            coef[n:n + 1, :] = parts[n] / total
        columns = coef[...].T
        joined = jnp.zeros((SLOTS, HD), F32)
        for n in range(NXY):
            joined = joined + orecv[half, n].astype(F32) * columns[0:SLOTS, n:n + 1]
        owned = jnp.dot(to_owners, joined.astype(BF16), preferred_element_type=F32)
        fbuf[NP * half:NP * half + NP] = owned.astype(BF16).reshape(NP, 16, HD)
        for pos in range(NP * half, NP * half + NP):

            @pl.when(pos != own)
            def _():
                fcopy(pos, h).start()

            @pl.when(pos == own)
            def _():
                frecv[h] = fbuf[pos]

    def assemble(h2):
        fstage[h2] = frecv[h2].astype(F32)
        for j in range(GH):
            columns = pl.ds(pl.multiple_of(h2 * GW + j * HD, HD), HD)
            fout[:, columns] = fstage[h2, 3 * j:3 * j + 3, :]

    assemble(h)

    @pl.loop(0, NZ - 1)
    def _(k):
        zcopy(zfar(k), z, z).wait_send()

    for d in REACH:
        wcopy(d).wait_send()

    for a in range(2):
        ccopy(a).wait_send()

    @pl.loop(1, NXY)
    def _(k):
        xy2 = lax.rem(xy + k, NXY)
        for half in range(2):
            pcopy(qall.at[half, xy], qall.at[half, xy], xy2, half, xy2, qs, qr).wait_send()
            pcopy(obuf.at[half, xy2], orecv.at[half, xy], xy2, half, xy2, osm, orm).wait_send()

    for d in reversed(REACH):
        h2 = lax.rem(near(-d), NL)
        pltpu.make_async_remote_copy(
            src_ref=fbuf.at[0], dst_ref=frecv.at[h2], send_sem=fs.at[0], recv_sem=fr.at[h2],
            device_id=zdev(near(1)), device_id_type=MESH).wait_recv()
        assemble(h2)

    out_ref[...] = fout[...].astype(BF16)

    for pos in range(NL):

        @pl.when(pos != own)
        def _():
            fcopy(pos, h).wait_send()


def on_device(query, delta_key, delta_value, base_key, base_value):
    vmem = pl.BlockSpec(memory_space=pltpu.VMEM)
    hbm = pl.BlockSpec(memory_space=pl.ANY)
    dma = pltpu.SemaphoreType.DMA
    return pl.pallas_call(
        kernel,
        out_shape=jax.ShapeDtypeStruct(query.shape, BF16),
        in_specs=[hbm] * 5,
        out_specs=vmem,
        scratch_shapes=[
            pltpu.VMEM((NL, 2, 16, HD), F32),
            pltpu.VMEM((NL, 16, HD), F32),
            pltpu.VMEM((NL, 2, 16, HD), BF16),
            pltpu.VMEM((NL, 16, HD), BF16),
            pltpu.VMEM((NZ, 2, 16, HD), BF16),
            pltpu.VMEM((NL, 16, HD), BF16),
            pltpu.VMEM(((GH + 1) * ZT, NZ * 16), BF16),
            pltpu.VMEM((2, 2, 32, GW), BF16),
            pltpu.VMEM((2, 2, 32, GW), F32),
            pltpu.VMEM((NC, GH, ZT, HD), BF16),
            pltpu.VMEM((NC, GH, ZT, HD), BF16),
            pltpu.VMEM((2, NXY, SLOTS, HD), BF16),
            pltpu.VMEM((HD, GH * KEYS), BF16),
            pltpu.VMEM((NXY // QUAD, GH * KEYS, QUAD * SLOTS), BF16),
            pltpu.VMEM((NXY // QUAD, 8, QUAD * SLOTS), F32),
            pltpu.VMEM((2, NXY, SLOTS, HD), BF16),
            pltpu.VMEM((2, NXY, SLOTS, HD), BF16),
            pltpu.VMEM((NXY, HD), F32),
            pltpu.VMEM((NL, 16, HD), BF16),
            pltpu.VMEM((NL, 16, HD), BF16),
            pltpu.VMEM((NL, 16, HD), F32),
            pltpu.VMEM(query.shape, F32),
            pltpu.VMEM(query.shape, BF16),
            pltpu.VMEM(query.shape, F32),
            pltpu.VMEM(query.shape, F32),
            dma((3,)), dma((4,)), dma((NZ,)), dma((NZ,)), dma((NL,)), dma((NL,)), dma((2,)), dma((2,)),
            dma((2, NXY)), dma((2, NXY)), dma((2, NXY)), dma((2, NXY)), dma((NL,)), dma((NL,)),
        ],
        compiler_params=pltpu.CompilerParams(
            collective_id=0, has_side_effects=True, vmem_limit_bytes=60 * 1024 * 1024),
    )(query, delta_key, delta_value, base_key, base_value)


def solution(mesh):
    rows = P(("patch", "head"), None)
    cols = P(None, "head")
    return jax.shard_map(
        on_device, mesh=mesh, in_specs=(rows, rows, rows, cols, cols), out_specs=rows, check_vma=False)
```
